128 devices in a mesh: tile: 32 (over z, x, core), pos: 4 (over y).
Axes of the slice: x: 4, y: 4, z: 4, core: 2. Of those that a mesh axis runs over, the one named last changes fastest.
Arguments:
- object_tiles: bfloat16 [32, 2, 512, 512], P('tile', None, 'pos'), may hold values from -4.1875 to 4.1875
- probe: float32 [2, 256, 256], replicated, may hold values from -4.2 to 4.2
- frames: bfloat16 [2048, 256, 256], P(('tile', 'pos')), may hold values from 0 to 60, as said below
- offsets: int32 [2, 2048], P(None, ('tile', 'pos')), may hold values from 1 to 511
Outputs:
- shifts: float32 [2, 2048], P(None, ('tile', 'pos'))
- losses: float32 [2048], P(('tile', 'pos'))
The draws below stay inside these ranges and needn't reach their ends.
Inputs may be any that keep to these rules, and one draw needn't show every extreme that they name: `frames`: amplitudes are not negative.
All inputs are finite; a program needn't handle non-finite values.
Results may differ from the reference program's by a relative error of at most 0.0097.
Values may be sent and summed in bfloat16 or wider, within the bound.
No kernel may reach another device: no remote copies, remote signals or barrier semaphores. Data moves between devices by JAX's collectives and lax.ppermute only.
A program may use at most 128 MiB of HBM per device.

```python
import math
import jax
import jax.numpy as jnp
from jax import lax

PROBE = 256
GC = 4
POS_DEV = 16
CORE = 512
TILES = 32
POSITIONS = 2048
N_TILE = 32
N_POS = 4


def draw_frames(key, part):
    ramp_scale = 1.0 + 2.0 * jnp.arange(POSITIONS, dtype=jnp.float32) / (POSITIONS - 1)
    normal_base = jax.random.normal(jax.random.fold_in(key, 5), (POSITIONS, PROBE, PROBE), jnp.float32)
    amplitude = jnp.minimum(jnp.abs(normal_base), 5.0) * ramp_scale[:, None, None]
    return amplitude.astype(jnp.bfloat16)


def with_ends(values, key, low, high):
    extent = values.shape
    index_at = [jax.random.randint(jax.random.fold_in(key, axis), (), 0, extent[axis]) for axis in range(len(extent))]
    values = values.at[tuple(index_at)].set(low)
    longest = extent.index(max(extent))
    index_at[longest] = (index_at[longest] + 1) % extent[longest]
    return values.at[tuple(index_at)].set(high)


def levels(stream_key, extent, split, least, high):
    loudness, own = 1.0, jax.random.fold_in(stream_key, 6)
    for dim, blocks in split:
        heights = jnp.exp(jax.random.uniform(jax.random.fold_in(own, dim), (blocks,), jnp.float32, least / len(split), high / len(split)))
        loudness = loudness * jnp.repeat(heights, extent[dim] // blocks).reshape([-1 if axis == dim else 1 for axis in range(len(extent))])
    return loudness


def centred(stream_key, dims, deviation, limit, split=(), kind=jnp.bfloat16):
    result = deviation * jax.random.normal(stream_key, dims, jnp.float32)
    if split:
        result = result * levels(stream_key, dims, split, -0.22, 0.18)
    return jnp.clip(result, -limit, limit).astype(kind)


def setup_inputs(seed: int = 0) -> dict:
    key_of = jax.random.split(jax.random.key(seed), 5)
    object_tiles = centred(key_of[0], (TILES, 2, CORE, CORE), 0.7, 4.1875, ((0, 32), (2, 4)))
    probe = centred(key_of[1], (2, PROBE, PROBE), 0.7, 4.2, (), jnp.float32)
    frames = draw_frames(jax.random.fold_in(key_of[4], 71), 0)
    offsets = with_ends(jax.random.randint(key_of[3], (2, POSITIONS), 1, CORE), jax.random.fold_in(key_of[3], 1), 1, CORE - 1).astype(jnp.int32)
    return dict(object_tiles=object_tiles, probe=probe, frames=frames, offsets=offsets)


def dft_tables(length_n):
    indices = jnp.arange(length_n, dtype=jnp.int32)
    products_mod = indices[:, None] * indices[None, :] % length_n
    angles = products_mod.astype(jnp.float32) * (2.0 * math.pi / length_n)
    factor = 1.0 / math.sqrt(length_n)
    return ((jnp.cos(angles) * factor).astype(jnp.bfloat16), (jnp.sin(angles) * factor).astype(jnp.bfloat16))

def matmul(left_m, right_m):
    return jnp.dot(left_m, right_m, preferred_element_type=jnp.float32)

def refine_ref(window, probe, detector, cosine_table, sine_table):
    window_f = window.astype(jnp.float32)
    patch = window_f[:, 1:-1, 1:-1]
    along_row = 0.5 * (window_f[:, 2:, 1:-1] - window_f[:, :-2, 1:-1])
    along_col = 0.5 * (window_f[:, 1:-1, 2:] - window_f[:, 1:-1, :-2])
    exit_re = (probe[0] * patch[0] - probe[1] * patch[1]).astype(jnp.bfloat16)
    exit_im = (probe[0] * patch[1] + probe[1] * patch[0]).astype(jnp.bfloat16)
    half_re = (matmul(cosine_table, exit_re) + matmul(sine_table, exit_im)).astype(jnp.bfloat16)
    half_im = (matmul(cosine_table, exit_im) - matmul(sine_table, exit_re)).astype(jnp.bfloat16)
    far_re = matmul(half_re, cosine_table) + matmul(half_im, sine_table)
    far_im = matmul(half_im, cosine_table) - matmul(half_re, sine_table)
    magnitude = jnp.sqrt(far_re * far_re + far_im * far_im)
    keep_part = 1.0 - detector.astype(jnp.float32) / jnp.maximum(magnitude, 0.25)
    resid_re = far_re * keep_part
    resid_im = far_im * keep_part
    loss_one = jnp.mean(resid_re * resid_re + resid_im * resid_im)
    round_re = resid_re.astype(jnp.bfloat16)
    round_im = resid_im.astype(jnp.bfloat16)
    inner_re = (matmul(cosine_table, round_re) - matmul(sine_table, round_im)).astype(jnp.bfloat16)
    inner_im = (matmul(cosine_table, round_im) + matmul(sine_table, round_re)).astype(jnp.bfloat16)
    wave_re = matmul(inner_re, cosine_table) - matmul(inner_im, sine_table)
    wave_im = matmul(inner_im, cosine_table) + matmul(inner_re, sine_table)

    def slope_of(derived):
        probed_re = probe[0] * derived[0] - probe[1] * derived[1]
        probed_im = probe[0] * derived[1] + probe[1] * derived[0]
        return jnp.sum(wave_re * probed_re + wave_im * probed_im)
    return (jnp.stack([slope_of(along_row), slope_of(along_col)]), loss_one)

def reference(object_tiles, probe, frames, offsets):
    region_rows = N_TILE // GC
    region_grid = object_tiles.reshape(region_rows, GC, 2, CORE, CORE)
    full_object = region_grid.transpose(2, 0, 3, 1, 4).reshape(2, region_rows * CORE, GC * CORE)
    margin = PROBE // 2
    padded = jnp.pad(full_object, ((0, 0), (margin, margin), (margin, margin)))
    indices = jnp.arange(POSITIONS, dtype=jnp.int32)
    region_of = indices // (POS_DEV * N_POS)
    starts_row = region_of // GC * CORE + offsets[0] - 1
    starts_col = region_of % GC * CORE + offsets[1] - 1
    cosine_table, sine_table = dft_tables(PROBE)

    def refine_at(position):
        detector, start_row, start_col = position
        window = lax.dynamic_slice(padded, (jnp.zeros((), jnp.int32), start_row.astype(jnp.int32), start_col.astype(jnp.int32)), (2, PROBE + 2, PROBE + 2))
        return refine_ref(window, probe, detector, cosine_table, sine_table)
    slopes, losses = lax.map(refine_at, (frames, starts_row, starts_col))
    total_sq = jnp.sum(slopes * slopes)
    norm_scale = jnp.sqrt(total_sq / POSITIONS + 1e-06)
    return ((-slopes / norm_scale).T, losses)
```

```python
import functools
import math

import jax
import jax.numpy as jnp
import numpy as np
from jax import lax
from jax.experimental import pallas as pl
from jax.experimental.pallas import tpu as pltpu
from jax.sharding import Mesh
from jax.sharding import PartitionSpec as P

PROBE = 256
MARGIN = PROBE // 2
LANES = 128
GC = 4
TILE = ("tile_0", "tile_1", "tile_2")
TILE_POS = ("tile_0", "tile_1", "tile_2", "pos")


def passed_along(x, axis, by):
    devices = lax.axis_size(axis)
    pairs = [(i, i + by) for i in range(devices) if 0 <= i + by < devices]
    return lax.ppermute(x, axis, pairs)


def round_ring(x, axis, by):
    devices = lax.axis_size(axis)
    return lax.ppermute(x, axis, [(i, (i + by) % devices) for i in range(devices)])


def dft_tables(length_n):
    indices = jnp.arange(length_n, dtype=jnp.int32)
    products_mod = indices[:, None] * indices[None, :] % length_n
    angles = products_mod.astype(jnp.float32) * (2.0 * math.pi / length_n)
    factor = 1.0 / math.sqrt(length_n)
    return (
        (jnp.cos(angles) * factor).astype(jnp.bfloat16),
        (jnp.sin(angles) * factor).astype(jnp.bfloat16),
    )


def refine_kernel(
    offsets_ref, padded_ref, probe_ref, frames_ref, forth_ref, back_ref, sums_ref,
    tile_ref, slant_ref, window_ref, across_ref, exit_ref, half_ref, far_ref, resid_ref, inner_ref, wave_ref,
):
    n = PROBE
    side = padded_ref.shape[1]
    blocks = side // LANES
    positions = frames_ref.shape[0]
    lane = lax.broadcasted_iota(jnp.int32, (LANES, LANES), 1)

    for part in range(2):
        for block in range(blocks):
            for row in range(0, side, LANES):
                tile_ref[part, block, pl.ds(row, LANES), :] = padded_ref[
                    part, pl.ds(row, LANES), pl.ds(block * LANES, LANES)
                ].astype(jnp.float32)

    for part in range(2):
        for block in range(blocks):
            for row in range(0, side, LANES):
                here = tile_ref[part, block, pl.ds(row, LANES), :]
                after = tile_ref[part, min(block + 1, blocks - 1), pl.ds(row, LANES), :]
                before = tile_ref[part, max(block - 1, 0), pl.ds(row, LANES), :]
                following = pltpu.roll(jnp.where(lane == 0, after, here), LANES - 1, 1)
                preceding = pltpu.roll(jnp.where(lane == LANES - 1, before, here), 1, 1)
                slant_ref[part, block, pl.ds(row, LANES), :] = following - preceding

    def one(position, carry):
        start_row = offsets_ref[0, position]
        start_col = offsets_ref[1, position]
        block = start_col // LANES
        rest = start_col % LANES
        shift = lax.rem(LANES - rest, LANES)
        for part in range(2):
            for row, rows in ((0, 64), (64, 64), (128, 64), (192, 64), (256, 8)):
                kept = lane[:rows] < LANES - rest
                rolled = [
                    pltpu.roll(tile_ref[part, block + b, pl.ds(start_row - 1 + row, rows), :], shift, 1)
                    for b in range(3)
                ]
                for b in range(2):
                    window_ref[part, b, pl.ds(row, rows), :] = jnp.where(kept, rolled[b], rolled[b + 1])
                if rows == 64:
                    rolled = [
                        pltpu.roll(slant_ref[part, block + b, pl.ds(start_row + row, rows), :], shift, 1)
                        for b in range(3)
                    ]
                    for b in range(2):
                        across_ref[part, b, pl.ds(row, rows), :] = jnp.where(kept, rolled[b], rolled[b + 1])
        for row in range(0, n, 64):
            for b in range(2):
                cols = pl.ds(b * LANES, LANES)
                patch_re = window_ref[0, b, pl.ds(row + 1, 64), :]
                patch_im = window_ref[1, b, pl.ds(row + 1, 64), :]
                probe_re = probe_ref[0, pl.ds(row, 64), cols]
                probe_im = probe_ref[1, pl.ds(row, 64), cols]
                exit_ref[pl.ds(row, 64), cols] = (probe_re * patch_re - probe_im * patch_im).astype(jnp.bfloat16)
                exit_ref[pl.ds(n + row, 64), cols] = (probe_re * patch_im + probe_im * patch_re).astype(jnp.bfloat16)

        half = jnp.dot(forth_ref[...], exit_ref[...], preferred_element_type=jnp.float32)
        half_ref[:, :n] = half[:n].astype(jnp.bfloat16)
        half_ref[:, n:] = half[n:].astype(jnp.bfloat16)
        far_ref[...] = jnp.dot(half_ref[...], back_ref[...], preferred_element_type=jnp.float32)
        loss = jnp.zeros((8, LANES), jnp.float32)
        for row in range(0, n, 64):
            for b in range(2):
                far_re = far_ref[pl.ds(row, 64), pl.ds(b * LANES, LANES)]
                far_im = far_ref[pl.ds(row, 64), pl.ds(n + b * LANES, LANES)]
                frame = frames_ref[position, pl.ds(row, 64), pl.ds(b * LANES, LANES)].astype(jnp.float32)
                inverse = jnp.minimum(lax.rsqrt(far_re * far_re + far_im * far_im), 4.0)
                keep = 1.0 - frame * inverse
                resid_re = far_re * keep
                resid_im = far_im * keep
                loss += jnp.sum((resid_re * resid_re + resid_im * resid_im).reshape(8, 8, LANES), axis=0)
                resid_ref[pl.ds(row, 64), pl.ds(b * LANES, LANES)] = resid_re.astype(jnp.bfloat16)
                resid_ref[pl.ds(n + row, 64), pl.ds(b * LANES, LANES)] = resid_im.astype(jnp.bfloat16)
        inner = jnp.dot(back_ref[...], resid_ref[...], preferred_element_type=jnp.float32)
        inner_ref[:, :n] = inner[:n].astype(jnp.bfloat16)
        inner_ref[:, n:] = inner[n:].astype(jnp.bfloat16)
        wave_ref[...] = jnp.dot(inner_ref[...], forth_ref[...], preferred_element_type=jnp.float32)
        slope_row = jnp.zeros((8, LANES), jnp.float32)
        slope_col = jnp.zeros((8, LANES), jnp.float32)
        for row in range(0, n, 64):
            for b in range(2):
                cols = pl.ds(b * LANES, LANES)
                wave_re = wave_ref[pl.ds(row, 64), cols]
                wave_im = wave_ref[pl.ds(row, 64), pl.ds(n + b * LANES, LANES)]
                probe_re = probe_ref[0, pl.ds(row, 64), cols]
                probe_im = probe_ref[1, pl.ds(row, 64), cols]
                pull_re = wave_re * probe_re + wave_im * probe_im
                pull_im = wave_im * probe_re - wave_re * probe_im
                down_re = window_ref[0, b, pl.ds(row + 2, 64), :] - window_ref[0, b, pl.ds(row, 64), :]
                down_im = window_ref[1, b, pl.ds(row + 2, 64), :] - window_ref[1, b, pl.ds(row, 64), :]
                slope_row += jnp.sum((pull_re * down_re + pull_im * down_im).reshape(8, 8, LANES), axis=0)
                slant_re = across_ref[0, b, pl.ds(row, 64), :]
                slant_im = across_ref[1, b, pl.ds(row, 64), :]
                slope_col += jnp.sum((pull_re * slant_re + pull_im * slant_im).reshape(8, 8, LANES), axis=0)
        sums_ref[0, position] = slope_row
        sums_ref[1, position] = slope_col
        sums_ref[2, position] = loss
        return carry

    lax.fori_loop(0, positions, one, 0)


def refine(padded, probe, frames, offsets):
    n = PROBE
    positions = frames.shape[0]
    side = padded.shape[1]
    blocks = side // LANES
    cosine, sine = dft_tables(n)
    forth = jnp.concatenate(
        [jnp.concatenate([cosine, sine], axis=1), jnp.concatenate([-sine, cosine], axis=1)], axis=0
    )
    back = jnp.concatenate(
        [jnp.concatenate([cosine, -sine], axis=1), jnp.concatenate([sine, cosine], axis=1)], axis=0
    )
    vmem = pl.BlockSpec(memory_space=pltpu.VMEM)
    return pl.pallas_call(
        refine_kernel,
        out_shape=jax.ShapeDtypeStruct((3, positions, 8, LANES), jnp.float32),
        in_specs=[pl.BlockSpec(memory_space=pltpu.SMEM)] + [vmem] * 5,
        out_specs=vmem,
        scratch_shapes=[
            pltpu.VMEM((2, blocks, side + 8, LANES), jnp.float32),
            pltpu.VMEM((2, blocks, side, LANES), jnp.float32),
            pltpu.VMEM((2, 2, n + 8, LANES), jnp.float32),
            pltpu.VMEM((2, 2, n, LANES), jnp.float32),
            pltpu.VMEM((2 * n, n), jnp.bfloat16),
            pltpu.VMEM((n, 2 * n), jnp.bfloat16),
            pltpu.VMEM((n, 2 * n), jnp.float32),
            pltpu.VMEM((2 * n, n), jnp.bfloat16),
            pltpu.VMEM((n, 2 * n), jnp.bfloat16),
            pltpu.VMEM((n, 2 * n), jnp.float32),
        ],
        compiler_params=pltpu.CompilerParams(vmem_limit_bytes=48 * 1024 * 1024),
    )(offsets, padded, probe, frames, forth, back)


def local(object_tiles, probe, frames, offsets):
    quarter = object_tiles[0]
    place = lax.axis_index("pos")
    region_col = lax.axis_index(TILE) % GC
    below = round_ring(quarter, "pos", -1)
    above = round_ring(quarter, "pos", 1)
    across = round_ring(quarter, "pos", 2)
    turned = jnp.stack([quarter, below, across, above], axis=0)
    order = (jnp.arange(4) - place) % 4
    block = jnp.take(turned, order, axis=0)
    rows = block.transpose(1, 0, 2, 3).reshape(2, -1, quarter.shape[-1])
    north = passed_along(rows[:, -MARGIN:, :], TILE, GC)
    south = passed_along(rows[:, :MARGIN, :], TILE, -GC)
    tall = jnp.concatenate([north, rows, south], axis=1)
    west = passed_along(tall[:, :, -MARGIN:], TILE, 1)
    east = passed_along(tall[:, :, :MARGIN], TILE, -1)
    west = jnp.where(region_col > 0, west, jnp.zeros_like(west))
    east = jnp.where(region_col < GC - 1, east, jnp.zeros_like(east))
    padded = jnp.concatenate([west, tall, east], axis=2)
    sums = jnp.sum(refine(padded, probe, frames, offsets), axis=(2, 3))
    slopes = 0.5 * sums[:2]
    losses = sums[2] / (PROBE * PROBE)
    part = jnp.sum(slopes * slopes)
    devices = lax.axis_size(TILE) * lax.axis_size("pos")
    parts = lax.all_to_all(jnp.full((devices, LANES), part), TILE_POS, 0, 0, tiled=True)
    total_sq = jnp.sum(parts[:, 0])
    norm_scale = jnp.sqrt(total_sq / (frames.shape[0] * devices) + 1e-06)
    return (-slopes / norm_scale, losses)


def solution(mesh):
    split = Mesh(
        mesh.devices.reshape(4, 4, 2, mesh.shape["pos"]), ("tile_0", "tile_1", "tile_2", "pos")
    )
    return jax.shard_map(
        local,
        mesh=split,
        in_specs=(P(TILE, None, "pos", None), P(), P(TILE_POS, None, None), P(None, TILE_POS)),
        out_specs=(P(None, TILE_POS), P(TILE_POS)),
        check_vma=False,
    )
```

```python
import functools
import math

import jax
import jax.numpy as jnp
import numpy as np
from jax import lax
from jax.experimental import pallas as pl
from jax.experimental.pallas import tpu as pltpu
from jax.sharding import Mesh
from jax.sharding import PartitionSpec as P

PROBE = 256
MARGIN = PROBE // 2
LANES = 128
CHUNK = 16
KEPT = 6
GC = 4
TILE = ("tile_0", "tile_1", "tile_2")
TILE_POS = ("tile_0", "tile_1", "tile_2", "pos")


def from_rows(x, by):
    devices = lax.axis_size(TILE)
    return lax.ppermute(x, TILE, [(i, i + by) for i in range(devices) if 0 <= i + by < devices])


def from_side(x, by):
    devices = lax.axis_size(TILE)
    pairs = [(i, i + by) for i in range(devices) if 0 <= i % GC + by < GC]
    return lax.ppermute(x, TILE, pairs)


def round_ring(x, axis, by):
    devices = lax.axis_size(axis)
    return lax.ppermute(x, axis, [(i, (i + by) % devices) for i in range(devices)])


def stacked_tables(n):
    indices = np.arange(n, dtype=np.int32)
    angles = (indices[:, None] * indices[None, :] % n).astype(np.float32) * np.float32(2.0 * math.pi / n)
    factor = np.float32(1.0 / math.sqrt(n))
    cosine, sine = np.cos(angles) * factor, np.sin(angles) * factor
    forth = np.block([[cosine, sine], [-sine, cosine]]).astype(jnp.bfloat16)
    back = np.block([[cosine, -sine], [sine, cosine]]).astype(jnp.bfloat16)
    return jnp.asarray(forth), jnp.asarray(back)


def refine_kernel(offsets_ref, north_ref, south_ref, west_ref, east_ref, *refs):
    quarter_refs = refs[:4]
    probe_ref, frames_ref, forth_ref, back_ref, sums_ref, tile_ref, slant_ref, turned_ref = refs[4:12]
    slots = refs[12:]
    n = PROBE
    side = west_ref.shape[1]
    blocks = side // LANES
    positions = frames_ref.shape[0]
    kept_probes = turned_ref.shape[0]
    exits, halves, fars, resids, inners, waves = (slots[2 * i:2 * i + 2] for i in range(6))
    lane = lax.broadcasted_iota(jnp.int32, (LANES, LANES), 1)

    rows_here = LANES
    for part in range(2):
        for piece in range(blocks):
            if piece == 0:
                first, middle_ref = 0, north_ref
            elif piece == blocks - 1:
                first, middle_ref = side - rows_here, south_ref
            else:
                turned = lax.rem(offsets_ref[2, 0] + piece - 1, blocks - 2)
                first, middle_ref = pl.multiple_of((turned + 1) * rows_here, rows_here), quarter_refs[piece - 1]
            into = pl.ds(first, rows_here)
            aside = pl.ds(piece * rows_here, rows_here)
            tile_ref[part, 0, into, :] = west_ref[part, aside, :].astype(jnp.float32)
            tile_ref[part, blocks - 1, into, :] = east_ref[part, aside, :].astype(jnp.float32)
            for block in range(1, blocks - 1):
                tile_ref[part, block, into, :] = middle_ref[
                    part, :, pl.ds((block - 1) * LANES, LANES)
                ].astype(jnp.float32)
    for part in range(2):
        for block in range(blocks):
            for row in range(0, side, LANES):
                here = tile_ref[part, block, pl.ds(row, LANES), :]
                after = tile_ref[part, min(block + 1, blocks - 1), pl.ds(row, LANES), :]
                before = tile_ref[part, max(block - 1, 0), pl.ds(row, LANES), :]
                following = pltpu.roll(jnp.where(lane == 0, after, here), LANES - 1, 1)
                preceding = pltpu.roll(jnp.where(lane == LANES - 1, before, here), 1, 1)
                slant_ref[part, block, pl.ds(row, LANES), :] = following - preceding

    def cut(position, slot):
        start_row = offsets_ref[0, position]
        start_col = offsets_ref[1, position]
        block = start_col // LANES
        rest = start_col % LANES
        held = lax.rem(position, kept_probes)
        exit_ref = exits[slot]
        wrapped = lax.broadcasted_iota(jnp.int32, (CHUNK, LANES), 1) < rest

        def piece(row):
            turned = []
            for part in range(2):
                left = pltpu.roll(probe_ref[part, pl.ds(row, CHUNK), pl.ds(0, LANES)], rest, 1)
                right = pltpu.roll(probe_ref[part, pl.ds(row, CHUNK), pl.ds(LANES, LANES)], rest, 1)
                turned.append((jnp.where(wrapped, right, left), jnp.where(wrapped, left, right)))
                for b in range(2):
                    turned_ref[held, part, b, pl.ds(row, CHUNK), :] = turned[part][b]
            for b in range(2):
                cols = pl.ds(b * LANES, LANES)
                patch = [tile_ref[part, block + b, pl.ds(start_row + row, CHUNK), :] for part in range(2)]
                if b == 0:
                    patch = [jnp.where(wrapped, tile_ref[part, block + 2, pl.ds(start_row + row, CHUNK), :], patch[part]) for part in range(2)]
                probe_re, probe_im = turned[0][b], turned[1][b]
                exit_ref[pl.ds(row, CHUNK), cols] = (probe_re * patch[0] - probe_im * patch[1]).astype(jnp.bfloat16)
                exit_ref[pl.ds(n + row, CHUNK), cols] = (probe_re * patch[1] + probe_im * patch[0]).astype(jnp.bfloat16)

        return [functools.partial(piece, row) for row in range(0, n, CHUNK)]

    def products(left_ref, into_ref, right_ref, from_ref, slot, out_ref):
        def rows(i):
            into_ref[:, i * n:(i + 1) * n] = jnp.dot(
                left_ref[i * n:(i + 1) * n, :], from_ref[...], preferred_element_type=jnp.float32
            ).astype(jnp.bfloat16)

        def cols(i):
            out_ref[:, i * n:(i + 1) * n] = jnp.dot(
                into_ref[...], right_ref[:, i * n:(i + 1) * n], preferred_element_type=jnp.float32
            )

        return [functools.partial(rows, 0), functools.partial(rows, 1), functools.partial(cols, 0), functools.partial(cols, 1)]

    def forward(slot):
        return products(forth_ref, halves[slot], back_ref, exits[slot], slot, fars[slot])

    def backward(slot):
        return products(back_ref, inners[slot], forth_ref, resids[slot], slot, waves[slot])

    def compare(position, slot):
        far_ref, resid_ref = fars[slot], resids[slot]
        total = [jnp.zeros((8, LANES), jnp.float32)]

        def piece(row):
            for b in range(2):
                far_re = far_ref[pl.ds(row, CHUNK), pl.ds(b * LANES, LANES)]
                far_im = far_ref[pl.ds(row, CHUNK), pl.ds(n + b * LANES, LANES)]
                frame = frames_ref[position, pl.ds(row, CHUNK), pl.ds(b * LANES, LANES)].astype(jnp.float32)
                power = far_re * far_re + far_im * far_im
                keep = 1.0 - frame * jnp.minimum(lax.rsqrt(power), 4.0)
                total[0] += jnp.sum((power * (keep * keep)).reshape(CHUNK // 8, 8, LANES), axis=0)
                resid_ref[pl.ds(row, CHUNK), pl.ds(b * LANES, LANES)] = (far_re * keep).astype(jnp.bfloat16)
                resid_ref[pl.ds(n + row, CHUNK), pl.ds(b * LANES, LANES)] = (far_im * keep).astype(jnp.bfloat16)
            if row + CHUNK == n:
                sums_ref[2, position] = total[0]

        return [functools.partial(piece, row) for row in range(0, n, CHUNK)]

    def slopes(position, slot):
        wave_ref = waves[slot]
        start_row = offsets_ref[0, position]
        start_col = offsets_ref[1, position]
        block = start_col // LANES
        rest = start_col % LANES
        held = lax.rem(position, kept_probes)
        wrapped = lax.broadcasted_iota(jnp.int32, (CHUNK, LANES), 1) < rest
        total = [jnp.zeros((8, LANES), jnp.float32)] * 2

        def cut_of(ref, part, b, row):
            here = ref[part, block + b, pl.ds(row, CHUNK), :]
            if b == 0:
                here = jnp.where(wrapped, ref[part, block + 2, pl.ds(row, CHUNK), :], here)
            return here

        def piece(row):
            for b in range(2):
                wave_re = wave_ref[pl.ds(row, CHUNK), pl.ds(b * LANES, LANES)]
                wave_im = wave_ref[pl.ds(row, CHUNK), pl.ds(n + b * LANES, LANES)]
                probe_re = turned_ref[held, 0, b, pl.ds(row, CHUNK), :]
                probe_im = turned_ref[held, 1, b, pl.ds(row, CHUNK), :]
                pull_re = wave_re * probe_re + wave_im * probe_im
                pull_im = wave_im * probe_re - wave_re * probe_im
                down_re = cut_of(tile_ref, 0, b, start_row + 1 + row) - cut_of(tile_ref, 0, b, start_row - 1 + row)
                down_im = cut_of(tile_ref, 1, b, start_row + 1 + row) - cut_of(tile_ref, 1, b, start_row - 1 + row)
                total[0] += jnp.sum((pull_re * down_re + pull_im * down_im).reshape(CHUNK // 8, 8, LANES), axis=0)
                slant_re = cut_of(slant_ref, 0, b, start_row + row)
                slant_im = cut_of(slant_ref, 1, b, start_row + row)
                total[1] += jnp.sum((pull_re * slant_re + pull_im * slant_im).reshape(CHUNK // 8, 8, LANES), axis=0)
            if row + CHUNK == n:
                sums_ref[0, position] = total[0]
                sums_ref[1, position] = total[1]

        return [functools.partial(piece, row) for row in range(0, n, CHUNK)]

    def step(t, parity, stages):
        plain, matrix = [], []
        if 4 in stages: plain += slopes(t - 4, parity)
        if 2 in stages: plain += compare(t - 2, parity)
        if 0 in stages: plain += cut(t, parity)
        one = forward(1 - parity) if 1 in stages else []
        two = backward(1 - parity) if 3 in stages else []
        if one and two:
            matrix = [piece for both in zip(one, two) for piece in both]
        else:
            matrix = one + two
        done = 0
        for i, piece in enumerate(matrix):
            piece()
            upto = (i + 1) * len(plain) // len(matrix)
            for other in plain[done:upto]:
                other()
            done = upto
        for other in plain[done:]:
            other()

    for t in range(4):
        step(t, t % 2, range(t + 1))
    def pair(i, carry):
        t = 4 + 2 * i
        step(t, 0, range(5))
        step(t + 1, 1, range(5))
        return carry
    lax.fori_loop(0, (positions - 4) // 2, pair, 0)
    for t in range(positions, positions + 4):
        step(t, t % 2, range(t - positions + 1, 5))


def refine(offsets, north, south, west, east, quarters, probe, frames):
    n = PROBE
    positions = frames.shape[0]
    side = west.shape[1]
    blocks = side // LANES
    forth, back = stacked_tables(n)
    vmem = pl.BlockSpec(memory_space=pltpu.VMEM)
    slots = []
    for shape, dtype in (
        ((2 * n, n), jnp.bfloat16), ((n, 2 * n), jnp.bfloat16), ((n, 2 * n), jnp.float32),
        ((2 * n, n), jnp.bfloat16), ((n, 2 * n), jnp.bfloat16), ((n, 2 * n), jnp.float32),
    ):
        slots += [pltpu.VMEM(shape, dtype)] * 2
    return pl.pallas_call(
        refine_kernel,
        out_shape=jax.ShapeDtypeStruct((3, positions, 8, LANES), jnp.float32),
        in_specs=[pl.BlockSpec(memory_space=pltpu.SMEM)] + [vmem] * 12,
        out_specs=vmem,
        scratch_shapes=[
            pltpu.VMEM((2, blocks, side + 8, LANES), jnp.float32),
            pltpu.VMEM((2, blocks, side, LANES), jnp.float32),
            pltpu.VMEM((KEPT, 2, 2, n, LANES), jnp.float32),
        ] + slots,
        compiler_params=pltpu.CompilerParams(vmem_limit_bytes=56 * 1024 * 1024),
    )(offsets, north, south, west, east, *quarters, probe, frames, forth, back)


def local(object_tiles, probe, frames, offsets):
    quarter = object_tiles[0]
    place = lax.axis_index("pos")
    turned = [quarter, round_ring(quarter, "pos", -1), round_ring(quarter, "pos", 2), round_ring(quarter, "pos", 1)]

    def quarter_of(pos):
        at = lax.rem(pos - place + 4, 4)
        return jnp.where(at < 2, jnp.where(at == 0, turned[0], turned[1]), jnp.where(at == 2, turned[2], turned[3]))

    north = from_rows(quarter_of(3), GC)
    south = from_rows(quarter_of(0), -GC)
    pieces = [north, *turned, south]
    west = from_side(jnp.concatenate([piece[:, :, -MARGIN:] for piece in pieces], axis=1), 1)
    east = from_side(jnp.concatenate([piece[:, :, :MARGIN] for piece in pieces], axis=1), -1)
    with_place = jnp.concatenate([offsets, jnp.full((1, offsets.shape[1]), place, jnp.int32)], axis=0)
    sums = jnp.sum(refine(with_place, north, south, west, east, turned, probe, frames), axis=(2, 3))
    slopes = 0.5 * sums[:2]
    losses = sums[2] / (PROBE * PROBE)
    part = jnp.sum(slopes * slopes)
    devices = lax.axis_size(TILE) * lax.axis_size("pos")
    parts = lax.all_to_all(jnp.full((devices, LANES), part), TILE_POS, 0, 0, tiled=True)
    total_sq = jnp.sum(parts[:, 0])
    norm_scale = jnp.sqrt(total_sq / (frames.shape[0] * devices) + 1e-06)
    return (-slopes / norm_scale, losses)


def solution(mesh):
    split = Mesh(
        mesh.devices.reshape(4, 4, 2, mesh.shape["pos"]), ("tile_0", "tile_1", "tile_2", "pos")
    )
    return jax.shard_map(
        local,
        mesh=split,
        in_specs=(P(TILE, None, "pos", None), P(), P(TILE_POS, None, None), P(None, TILE_POS)),
        out_specs=(P(None, TILE_POS), P(TILE_POS)),
        check_vma=False,
    )
```

```python
import functools
import math

import jax
import jax.numpy as jnp
import numpy as np
from jax import lax
from jax.experimental import pallas as pl
from jax.experimental.pallas import tpu as pltpu
from jax.sharding import Mesh
from jax.sharding import PartitionSpec as P

PROBE = 256
MARGIN = PROBE // 2
LANES = 128
CHUNK = 16
KEPT = 6
GC = 4
TILE = ("tile_0", "tile_1", "tile_2")
TILE_POS = ("tile_0", "tile_1", "tile_2", "pos")


def up_and_down(x, down, up):
    regions, across = lax.axis_size(TILE), lax.axis_size("pos")
    pairs = [(i * across + down, (i + GC) * across + down) for i in range(regions - GC)]
    pairs += [(i * across + up, (i - GC) * across + up) for i in range(GC, regions)]
    return lax.ppermute(x, TILE_POS, pairs)


def from_side(x, by):
    devices = lax.axis_size(TILE)
    pairs = [(i, i + by) for i in range(devices) if 0 <= i % GC + by < GC]
    return lax.ppermute(x, TILE, pairs)


def round_ring(x, axis, by):
    devices = lax.axis_size(axis)
    return lax.ppermute(x, axis, [(i, (i + by) % devices) for i in range(devices)])


def stacked_tables(n):
    indices = np.arange(n, dtype=np.int32)
    angles = (indices[:, None] * indices[None, :] % n).astype(np.float32) * np.float32(2.0 * math.pi / n)
    factor = np.float32(1.0 / math.sqrt(n))
    cosine, sine = np.cos(angles) * factor, np.sin(angles) * factor
    forth = np.block([[cosine, sine], [-sine, cosine]]).astype(jnp.bfloat16)
    back = np.block([[cosine, -sine], [sine, cosine]]).astype(jnp.bfloat16)
    return jnp.asarray(forth), jnp.asarray(back)


def refine_kernel(offsets_ref, north_ref, south_ref, side_west_ref, side_east_ref, caps_west_ref, caps_east_ref, *refs):
    quarter_refs = refs[:4]
    probe_ref, frames_ref, forth_ref, back_ref, result_ref, part_ref, tile_ref, slant_ref, turned_ref, sums_ref = refs[4:14]
    slots = refs[14:]
    n = PROBE
    side = tile_ref.shape[2] - 8
    blocks = side // LANES
    positions = frames_ref.shape[0]
    kept_probes = turned_ref.shape[0]
    exits, halves, fars, resids, inners, waves = (slots[2 * i:2 * i + 2] for i in range(6))
    lane = lax.broadcasted_iota(jnp.int32, (LANES, LANES), 1)

    rows_here = LANES
    for part in range(2):
        for piece in range(blocks):
            if piece == 0:
                first, middle_ref = 0, north_ref
            elif piece == blocks - 1:
                first, middle_ref = side - rows_here, south_ref
            else:
                turned = lax.rem(offsets_ref[2, 0] + piece - 1, blocks - 2)
                first, middle_ref = pl.multiple_of((turned + 1) * rows_here, rows_here), quarter_refs[piece - 1]
            into = pl.ds(first, rows_here)
            if piece in (0, blocks - 1):
                west_ref, east_ref, aside = caps_west_ref, caps_east_ref, pl.ds(rows_here if piece else 0, rows_here)
            else:
                west_ref, east_ref, aside = side_west_ref, side_east_ref, pl.ds((piece - 1) * rows_here, rows_here)
            tile_ref[part, 0, into, :] = west_ref[part, aside, :].astype(jnp.float32)
            tile_ref[part, blocks - 1, into, :] = east_ref[part, aside, :].astype(jnp.float32)
            for block in range(1, blocks - 1):
                tile_ref[part, block, into, :] = middle_ref[
                    part, :, pl.ds((block - 1) * LANES, LANES)
                ].astype(jnp.float32)
    for part in range(2):
        for block in range(blocks):
            for row in range(0, side, LANES):
                here = tile_ref[part, block, pl.ds(row, LANES), :]
                after = tile_ref[part, min(block + 1, blocks - 1), pl.ds(row, LANES), :]
                before = tile_ref[part, max(block - 1, 0), pl.ds(row, LANES), :]
                following = pltpu.roll(jnp.where(lane == 0, after, here), LANES - 1, 1)
                preceding = pltpu.roll(jnp.where(lane == LANES - 1, before, here), 1, 1)
                slant_ref[part, block, pl.ds(row, LANES), :] = following - preceding

    def cut(position, slot):
        start_row = offsets_ref[0, position]
        start_col = offsets_ref[1, position]
        block = start_col // LANES
        rest = start_col % LANES
        held = lax.rem(position, kept_probes)
        exit_ref = exits[slot]
        wrapped = lax.broadcasted_iota(jnp.int32, (CHUNK, LANES), 1) < rest

        def piece(row):
            turned = []
            for part in range(2):
                left = pltpu.roll(probe_ref[part, pl.ds(row, CHUNK), pl.ds(0, LANES)], rest, 1)
                right = pltpu.roll(probe_ref[part, pl.ds(row, CHUNK), pl.ds(LANES, LANES)], rest, 1)
                turned.append((jnp.where(wrapped, right, left), jnp.where(wrapped, left, right)))
                for b in range(2):
                    turned_ref[held, part, b, pl.ds(row, CHUNK), :] = turned[part][b]
            for b in range(2):
                cols = pl.ds(b * LANES, LANES)
                patch = [tile_ref[part, block + b, pl.ds(start_row + row, CHUNK), :] for part in range(2)]
                if b == 0:
                    patch = [jnp.where(wrapped, tile_ref[part, block + 2, pl.ds(start_row + row, CHUNK), :], patch[part]) for part in range(2)]
                probe_re, probe_im = turned[0][b], turned[1][b]
                exit_ref[pl.ds(row, CHUNK), cols] = (probe_re * patch[0] - probe_im * patch[1]).astype(jnp.bfloat16)
                exit_ref[pl.ds(n + row, CHUNK), cols] = (probe_re * patch[1] + probe_im * patch[0]).astype(jnp.bfloat16)

        return [functools.partial(piece, row) for row in range(0, n, CHUNK)]

    def products(left_ref, into_ref, right_ref, from_ref, slot, out_ref):
        def rows(i):
            into_ref[:, i * n:(i + 1) * n] = jnp.dot(
                left_ref[i * n:(i + 1) * n, :], from_ref[...], preferred_element_type=jnp.float32
            ).astype(jnp.bfloat16)

        def cols(i):
            out_ref[:, i * n:(i + 1) * n] = jnp.dot(
                into_ref[...], right_ref[:, i * n:(i + 1) * n], preferred_element_type=jnp.float32
            )

        return [functools.partial(rows, 0), functools.partial(rows, 1), functools.partial(cols, 0), functools.partial(cols, 1)]

    def forward(slot):
        return products(forth_ref, halves[slot], back_ref, exits[slot], slot, fars[slot])

    def backward(slot):
        return products(back_ref, inners[slot], forth_ref, resids[slot], slot, waves[slot])

    def compare(position, slot):
        far_ref, resid_ref = fars[slot], resids[slot]
        total = [jnp.zeros((8, LANES), jnp.float32)]

        def piece(row):
            for b in range(2):
                far_re = far_ref[pl.ds(row, CHUNK), pl.ds(b * LANES, LANES)]
                far_im = far_ref[pl.ds(row, CHUNK), pl.ds(n + b * LANES, LANES)]
                frame = frames_ref[position, pl.ds(row, CHUNK), pl.ds(b * LANES, LANES)].astype(jnp.float32)
                power = far_re * far_re + far_im * far_im
                keep = 1.0 - frame * jnp.minimum(lax.rsqrt(power), 4.0)
                total[0] += jnp.sum((power * (keep * keep)).reshape(CHUNK // 8, 8, LANES), axis=0)
                resid_ref[pl.ds(row, CHUNK), pl.ds(b * LANES, LANES)] = (far_re * keep).astype(jnp.bfloat16)
                resid_ref[pl.ds(n + row, CHUNK), pl.ds(b * LANES, LANES)] = (far_im * keep).astype(jnp.bfloat16)
            if row + CHUNK == n:
                sums_ref[2, position] = total[0]

        return [functools.partial(piece, row) for row in range(0, n, CHUNK)]

    def slopes(position, slot):
        wave_ref = waves[slot]
        start_row = offsets_ref[0, position]
        start_col = offsets_ref[1, position]
        block = start_col // LANES
        rest = start_col % LANES
        held = lax.rem(position, kept_probes)
        wrapped = lax.broadcasted_iota(jnp.int32, (CHUNK, LANES), 1) < rest
        total = [jnp.zeros((8, LANES), jnp.float32)] * 2

        def cut_of(ref, part, b, row):
            here = ref[part, block + b, pl.ds(row, CHUNK), :]
            if b == 0:
                here = jnp.where(wrapped, ref[part, block + 2, pl.ds(row, CHUNK), :], here)
            return here

        def piece(row):
            for b in range(2):
                wave_re = wave_ref[pl.ds(row, CHUNK), pl.ds(b * LANES, LANES)]
                wave_im = wave_ref[pl.ds(row, CHUNK), pl.ds(n + b * LANES, LANES)]
                probe_re = turned_ref[held, 0, b, pl.ds(row, CHUNK), :]
                probe_im = turned_ref[held, 1, b, pl.ds(row, CHUNK), :]
                pull_re = wave_re * probe_re + wave_im * probe_im
                pull_im = wave_im * probe_re - wave_re * probe_im
                down_re = cut_of(tile_ref, 0, b, start_row + 1 + row) - cut_of(tile_ref, 0, b, start_row - 1 + row)
                down_im = cut_of(tile_ref, 1, b, start_row + 1 + row) - cut_of(tile_ref, 1, b, start_row - 1 + row)
                total[0] += jnp.sum((pull_re * down_re + pull_im * down_im).reshape(CHUNK // 8, 8, LANES), axis=0)
                slant_re = cut_of(slant_ref, 0, b, start_row + row)
                slant_im = cut_of(slant_ref, 1, b, start_row + row)
                total[1] += jnp.sum((pull_re * slant_re + pull_im * slant_im).reshape(CHUNK // 8, 8, LANES), axis=0)
            if row + CHUNK == n:
                sums_ref[0, position] = total[0]
                sums_ref[1, position] = total[1]

        return [functools.partial(piece, row) for row in range(0, n, CHUNK)]

    def step(t, parity, stages):
        plain, matrix = [], []
        if 4 in stages: plain += slopes(t - 4, parity)
        if 2 in stages: plain += compare(t - 2, parity)
        if 0 in stages: plain += cut(t, parity)
        one = forward(1 - parity) if 1 in stages else []
        two = backward(1 - parity) if 3 in stages else []
        if one and two:
            matrix = [piece for both in zip(one, two) for piece in both]
        else:
            matrix = one + two
        done = 0
        for i, piece in enumerate(matrix):
            piece()
            upto = (i + 1) * len(plain) // len(matrix)
            for other in plain[done:upto]:
                other()
            done = upto
        for other in plain[done:]:
            other()

    for t in range(4):
        step(t, t % 2, range(t + 1))
    def pair(i, carry):
        t = 4 + 2 * i
        step(t, 0, range(5))
        step(t + 1, 1, range(5))
        return carry
    lax.fori_loop(0, (positions - 4) // 2, pair, 0)
    for t in range(positions, positions + 4):
        step(t, t % 2, range(t - positions + 1, 5))

    sums = jnp.sum(jnp.sum(sums_ref[...], axis=2), axis=2, keepdims=True)
    slope = 0.5 * sums[:2]
    part_ref[...] = jnp.full(part_ref.shape, jnp.sum(slope * slope))
    at = lax.broadcasted_iota(jnp.int32, (positions, LANES), 0) == lax.broadcasted_iota(jnp.int32, (positions, LANES), 1)
    for i, value in enumerate((slope[0], slope[1], sums[2] * (1.0 / (n * n)))):
        result_ref[i:i + 1, :] = jnp.sum(jnp.where(at, value, 0.0), axis=0, keepdims=True)


def scale_kernel(result_ref, parts_ref, shifts_ref, *, count):
    total = jnp.sum(jnp.sum(parts_ref[...], axis=0, keepdims=True)[:, :1])
    scale = 1.0 / jnp.sqrt(jnp.full((2, LANES), total * (1.0 / count) + 1e-06))
    shifts_ref[...] = (-result_ref[0:2, :] * scale)[:, :shifts_ref.shape[1]]


def refine(offsets, caps, side_strips, cap_strips, quarters, probe, frames, devices):
    n = PROBE
    positions = frames.shape[0]
    blocks = len(quarters) + 2
    side = blocks * LANES
    forth, back = stacked_tables(n)
    vmem = pl.BlockSpec(memory_space=pltpu.VMEM)
    slots = []
    for shape, dtype in (
        ((2 * n, n), jnp.bfloat16), ((n, 2 * n), jnp.bfloat16), ((n, 2 * n), jnp.float32),
        ((2 * n, n), jnp.bfloat16), ((n, 2 * n), jnp.bfloat16), ((n, 2 * n), jnp.float32),
    ):
        slots += [pltpu.VMEM(shape, dtype)] * 2
    return pl.pallas_call(
        refine_kernel,
        out_shape=[jax.ShapeDtypeStruct((8, LANES), jnp.float32), jax.ShapeDtypeStruct((devices, LANES), jnp.float32)],
        in_specs=[pl.BlockSpec(memory_space=pltpu.SMEM)] + [vmem] * 14,
        out_specs=[vmem, vmem],
        scratch_shapes=[
            pltpu.VMEM((2, blocks, side + 8, LANES), jnp.float32),
            pltpu.VMEM((2, blocks, side, LANES), jnp.float32),
            pltpu.VMEM((KEPT, 2, 2, n, LANES), jnp.float32),
            pltpu.VMEM((3, positions, 8, LANES), jnp.float32),
        ] + slots,
        compiler_params=pltpu.CompilerParams(vmem_limit_bytes=56 * 1024 * 1024),
    )(offsets, *caps, *side_strips, *cap_strips, *quarters, probe, frames, forth, back)


def local(object_tiles, probe, frames, offsets):
    quarter = object_tiles[0]
    place = lax.axis_index("pos")
    turned = [quarter, round_ring(quarter, "pos", -1), round_ring(quarter, "pos", 2), round_ring(quarter, "pos", 1)]

    came = [
        up_and_down(quarter, 3, 0),
        up_and_down(turned[3], 0, 1),
        up_and_down(turned[1], 2, 3),
        up_and_down(turned[2], 1, 2),
    ]

    def strips(pieces):
        west = from_side(jnp.concatenate([piece[:, :, -MARGIN:] for piece in pieces], axis=1), 1)
        east = from_side(jnp.concatenate([piece[:, :, :MARGIN] for piece in pieces], axis=1), -1)
        return west, east

    def of_pos(order):
        return jnp.where(
            place < 2,
            jnp.where(place == 0, came[order[0]], came[order[1]]),
            jnp.where(place == 2, came[order[2]], came[order[3]]),
        )

    side_strips = strips(turned)
    caps = (of_pos((1, 3, 2, 0)), of_pos((0, 1, 3, 2)))
    cap_strips = strips(caps)
    with_place = jnp.concatenate([offsets, jnp.full((1, offsets.shape[1]), place, jnp.int32)], axis=0)
    devices = lax.axis_size(TILE) * lax.axis_size("pos")
    positions = frames.shape[0]
    result, part = refine(with_place, caps, side_strips, cap_strips, turned, probe, frames, devices)
    parts = lax.all_to_all(part, TILE_POS, 0, 0, tiled=True)
    vmem = pl.BlockSpec(memory_space=pltpu.VMEM)
    shifts = pl.pallas_call(
        functools.partial(scale_kernel, count=positions * devices),
        out_shape=jax.ShapeDtypeStruct((2, positions), jnp.float32),
        in_specs=[vmem, vmem],
        out_specs=vmem,
    )(result, parts)
    return (shifts, result[2, :positions])


def solution(mesh):
    split = Mesh(
        mesh.devices.reshape(4, 4, 2, mesh.shape["pos"]), ("tile_0", "tile_1", "tile_2", "pos")
    )
    return jax.shard_map(
        local,
        mesh=split,
        in_specs=(P(TILE, None, "pos", None), P(), P(TILE_POS, None, None), P(None, TILE_POS)),
        out_specs=(P(None, TILE_POS), P(TILE_POS)),
        check_vma=False,
    )
```

```python
import functools
import math

import jax
import jax.numpy as jnp
import numpy as np
from jax import lax
from jax.experimental import pallas as pl
from jax.experimental.pallas import tpu as pltpu
from jax.sharding import Mesh
from jax.sharding import PartitionSpec as P

PROBE = 256
MARGIN = PROBE // 2
LANES = 128
CHUNK = 16
KEPT = 6
GC = 4
TILE = ("tile_0", "tile_1", "tile_2")
TILE_POS = ("tile_0", "tile_1", "tile_2", "pos")


def from_rows(x, by):
    devices = lax.axis_size(TILE)
    return lax.ppermute(x, TILE, [(i, i + by) for i in range(devices) if 0 <= i + by < devices])


def up_and_down(x, down, up):
    regions, across = lax.axis_size(TILE), lax.axis_size("pos")
    pairs = [(i * across + down, (i + GC) * across + down) for i in range(regions - GC)]
    pairs += [(i * across + up, (i - GC) * across + up) for i in range(GC, regions)]
    return lax.ppermute(x, TILE_POS, pairs)


def from_side(x, by):
    devices = lax.axis_size(TILE)
    pairs = [(i, i + by) for i in range(devices) if 0 <= i % GC + by < GC]
    return lax.ppermute(x, TILE, pairs)


def round_ring(x, axis, by):
    devices = lax.axis_size(axis)
    return lax.ppermute(x, axis, [(i, (i + by) % devices) for i in range(devices)])


def stacked_tables(n):
    indices = np.arange(n, dtype=np.int32)
    angles = (indices[:, None] * indices[None, :] % n).astype(np.float32) * np.float32(2.0 * math.pi / n)
    factor = np.float32(1.0 / math.sqrt(n))
    cosine, sine = np.cos(angles) * factor, np.sin(angles) * factor
    forth = np.block([[cosine, sine], [-sine, cosine]]).astype(jnp.bfloat16)
    back = np.block([[cosine, -sine], [sine, cosine]]).astype(jnp.bfloat16)
    return jnp.asarray(forth), jnp.asarray(back)


def refine_kernel(offsets_ref, north_ref, south_ref, side_west_ref, side_east_ref, north_sides_ref, south_sides_ref, *refs):
    quarter_refs = refs[:4]
    probe_ref, frames_ref, forth_ref, back_ref, result_ref, part_ref, tile_ref, slant_ref, turned_ref, sums_ref = refs[4:14]
    slots = refs[14:]
    n = PROBE
    side = tile_ref.shape[2] - 8
    blocks = side // LANES
    positions = frames_ref.shape[0]
    kept_probes = turned_ref.shape[0]
    exits, halves, fars, resids, inners, waves = (slots[2 * i:2 * i + 2] for i in range(6))
    lane = lax.broadcasted_iota(jnp.int32, (LANES, LANES), 1)

    rows_here = LANES
    for part in range(2):
        for piece in range(blocks):
            if piece == 0:
                first, middle_ref = 0, north_ref
            elif piece == blocks - 1:
                first, middle_ref = side - rows_here, south_ref
            else:
                turned = lax.rem(offsets_ref[2, 0] + piece - 1, blocks - 2)
                first, middle_ref = pl.multiple_of((turned + 1) * rows_here, rows_here), quarter_refs[piece - 1]
            into = pl.ds(first, rows_here)
            if piece in (0, blocks - 1):
                ends_ref = south_sides_ref if piece else north_sides_ref
                ends = ends_ref[part, :, :LANES], ends_ref[part, :, LANES:]
            else:
                aside = pl.ds((piece - 1) * rows_here, rows_here)
                ends = side_west_ref[part, aside, :], side_east_ref[part, aside, :]
            tile_ref[part, 0, into, :] = ends[0].astype(jnp.float32)
            tile_ref[part, blocks - 1, into, :] = ends[1].astype(jnp.float32)
            for block in range(1, blocks - 1):
                tile_ref[part, block, into, :] = middle_ref[
                    part, :, pl.ds((block - 1) * LANES, LANES)
                ].astype(jnp.float32)
    for part in range(2):
        for block in range(blocks):
            for row in range(0, side, LANES):
                here = tile_ref[part, block, pl.ds(row, LANES), :]
                after = tile_ref[part, min(block + 1, blocks - 1), pl.ds(row, LANES), :]
                before = tile_ref[part, max(block - 1, 0), pl.ds(row, LANES), :]
                following = pltpu.roll(jnp.where(lane == 0, after, here), LANES - 1, 1)
                preceding = pltpu.roll(jnp.where(lane == LANES - 1, before, here), 1, 1)
                slant_ref[part, block, pl.ds(row, LANES), :] = following - preceding

    def cut(position, slot):
        start_row = offsets_ref[0, position]
        start_col = offsets_ref[1, position]
        block = start_col // LANES
        rest = start_col % LANES
        held = lax.rem(position, kept_probes)
        exit_ref = exits[slot]
        wrapped = lax.broadcasted_iota(jnp.int32, (CHUNK, LANES), 1) < rest

        def piece(row):
            turned = []
            for part in range(2):
                left = pltpu.roll(probe_ref[part, pl.ds(row, CHUNK), pl.ds(0, LANES)], rest, 1)
                right = pltpu.roll(probe_ref[part, pl.ds(row, CHUNK), pl.ds(LANES, LANES)], rest, 1)
                turned.append((jnp.where(wrapped, right, left), jnp.where(wrapped, left, right)))
                for b in range(2):
                    turned_ref[held, part, b, pl.ds(row, CHUNK), :] = turned[part][b]
            for b in range(2):
                cols = pl.ds(b * LANES, LANES)
                patch = [tile_ref[part, block + b, pl.ds(start_row + row, CHUNK), :] for part in range(2)]
                if b == 0:
                    patch = [jnp.where(wrapped, tile_ref[part, block + 2, pl.ds(start_row + row, CHUNK), :], patch[part]) for part in range(2)]
                probe_re, probe_im = turned[0][b], turned[1][b]
                exit_ref[pl.ds(row, CHUNK), cols] = (probe_re * patch[0] - probe_im * patch[1]).astype(jnp.bfloat16)
                exit_ref[pl.ds(n + row, CHUNK), cols] = (probe_re * patch[1] + probe_im * patch[0]).astype(jnp.bfloat16)

        return [functools.partial(piece, row) for row in range(0, n, CHUNK)]

    def products(left_ref, into_ref, right_ref, from_ref, slot, out_ref):
        def rows(i):
            into_ref[:, i * n:(i + 1) * n] = jnp.dot(
                left_ref[i * n:(i + 1) * n, :], from_ref[...], preferred_element_type=jnp.float32
            ).astype(jnp.bfloat16)

        def cols(i):
            out_ref[:, i * n:(i + 1) * n] = jnp.dot(
                into_ref[...], right_ref[:, i * n:(i + 1) * n], preferred_element_type=jnp.float32
            )

        return [functools.partial(rows, 0), functools.partial(rows, 1), functools.partial(cols, 0), functools.partial(cols, 1)]

    def forward(slot):
        return products(forth_ref, halves[slot], back_ref, exits[slot], slot, fars[slot])

    def backward(slot):
        return products(back_ref, inners[slot], forth_ref, resids[slot], slot, waves[slot])

    def compare(position, slot):
        far_ref, resid_ref = fars[slot], resids[slot]
        total = [jnp.zeros((8, LANES), jnp.float32)]

        def piece(row):
            for b in range(2):
                far_re = far_ref[pl.ds(row, CHUNK), pl.ds(b * LANES, LANES)]
                far_im = far_ref[pl.ds(row, CHUNK), pl.ds(n + b * LANES, LANES)]
                frame = frames_ref[position, pl.ds(row, CHUNK), pl.ds(b * LANES, LANES)].astype(jnp.float32)
                power = far_re * far_re + far_im * far_im
                keep = 1.0 - frame * jnp.minimum(lax.rsqrt(power), 4.0)
                total[0] += jnp.sum((power * (keep * keep)).reshape(CHUNK // 8, 8, LANES), axis=0)
                resid_ref[pl.ds(row, CHUNK), pl.ds(b * LANES, LANES)] = (far_re * keep).astype(jnp.bfloat16)
                resid_ref[pl.ds(n + row, CHUNK), pl.ds(b * LANES, LANES)] = (far_im * keep).astype(jnp.bfloat16)
            if row + CHUNK == n:
                sums_ref[2, position] = total[0]

        return [functools.partial(piece, row) for row in range(0, n, CHUNK)]

    def slopes(position, slot):
        wave_ref = waves[slot]
        start_row = offsets_ref[0, position]
        start_col = offsets_ref[1, position]
        block = start_col // LANES
        rest = start_col % LANES
        held = lax.rem(position, kept_probes)
        wrapped = lax.broadcasted_iota(jnp.int32, (CHUNK, LANES), 1) < rest
        total = [jnp.zeros((8, LANES), jnp.float32)] * 2

        def cut_of(ref, part, b, row):
            here = ref[part, block + b, pl.ds(row, CHUNK), :]
            if b == 0:
                here = jnp.where(wrapped, ref[part, block + 2, pl.ds(row, CHUNK), :], here)
            return here

        def piece(row):
            for b in range(2):
                wave_re = wave_ref[pl.ds(row, CHUNK), pl.ds(b * LANES, LANES)]
                wave_im = wave_ref[pl.ds(row, CHUNK), pl.ds(n + b * LANES, LANES)]
                probe_re = turned_ref[held, 0, b, pl.ds(row, CHUNK), :]
                probe_im = turned_ref[held, 1, b, pl.ds(row, CHUNK), :]
                pull_re = wave_re * probe_re + wave_im * probe_im
                pull_im = wave_im * probe_re - wave_re * probe_im
                down_re = cut_of(tile_ref, 0, b, start_row + 1 + row) - cut_of(tile_ref, 0, b, start_row - 1 + row)
                down_im = cut_of(tile_ref, 1, b, start_row + 1 + row) - cut_of(tile_ref, 1, b, start_row - 1 + row)
                total[0] += jnp.sum((pull_re * down_re + pull_im * down_im).reshape(CHUNK // 8, 8, LANES), axis=0)
                slant_re = cut_of(slant_ref, 0, b, start_row + row)
                slant_im = cut_of(slant_ref, 1, b, start_row + row)
                total[1] += jnp.sum((pull_re * slant_re + pull_im * slant_im).reshape(CHUNK // 8, 8, LANES), axis=0)
            if row + CHUNK == n:
                sums_ref[0, position] = total[0]
                sums_ref[1, position] = total[1]

        return [functools.partial(piece, row) for row in range(0, n, CHUNK)]

    def step(t, parity, stages):
        plain, matrix = [], []
        if 4 in stages: plain += slopes(t - 4, parity)
        if 2 in stages: plain += compare(t - 2, parity)
        if 0 in stages: plain += cut(t, parity)
        one = forward(1 - parity) if 1 in stages else []
        two = backward(1 - parity) if 3 in stages else []
        if one and two:
            matrix = [piece for both in zip(one, two) for piece in both]
        else:
            matrix = one + two
        done = 0
        for i, piece in enumerate(matrix):
            piece()
            upto = (i + 1) * len(plain) // len(matrix)
            for other in plain[done:upto]:
                other()
            done = upto
        for other in plain[done:]:
            other()

    for t in range(4):
        step(t, t % 2, range(t + 1))
    def pair(i, carry):
        t = 4 + 2 * i
        step(t, 0, range(5))
        step(t + 1, 1, range(5))
        return carry
    lax.fori_loop(0, (positions - 4) // 2, pair, 0)
    for t in range(positions, positions + 4):
        step(t, t % 2, range(t - positions + 1, 5))

    sums = jnp.sum(jnp.sum(sums_ref[...], axis=2), axis=2, keepdims=True)
    slope = 0.5 * sums[:2]
    part_ref[...] = jnp.full(part_ref.shape, jnp.sum(slope * slope))
    at = lax.broadcasted_iota(jnp.int32, (positions, LANES), 0) == lax.broadcasted_iota(jnp.int32, (positions, LANES), 1)
    for i, value in enumerate((slope[0], slope[1], sums[2] * (1.0 / (n * n)))):
        result_ref[i:i + 1, :] = jnp.sum(jnp.where(at, value, 0.0), axis=0, keepdims=True)


def scale_kernel(result_ref, parts_ref, shifts_ref, *, count):
    total = jnp.sum(jnp.sum(parts_ref[...], axis=0, keepdims=True)[:, :1])
    scale = 1.0 / jnp.sqrt(jnp.full((2, LANES), total * (1.0 / count) + 1e-06))
    shifts_ref[...] = (-result_ref[0:2, :] * scale)[:, :shifts_ref.shape[1]]


def refine(offsets, caps, side_strips, cap_sides, quarters, probe, frames, devices):
    n = PROBE
    positions = frames.shape[0]
    blocks = len(quarters) + 2
    side = blocks * LANES
    forth, back = stacked_tables(n)
    vmem = pl.BlockSpec(memory_space=pltpu.VMEM)
    slots = []
    for shape, dtype in (
        ((2 * n, n), jnp.bfloat16), ((n, 2 * n), jnp.bfloat16), ((n, 2 * n), jnp.float32),
        ((2 * n, n), jnp.bfloat16), ((n, 2 * n), jnp.bfloat16), ((n, 2 * n), jnp.float32),
    ):
        slots += [pltpu.VMEM(shape, dtype)] * 2
    return pl.pallas_call(
        refine_kernel,
        out_shape=[jax.ShapeDtypeStruct((8, LANES), jnp.float32), jax.ShapeDtypeStruct((devices, LANES), jnp.float32)],
        in_specs=[pl.BlockSpec(memory_space=pltpu.SMEM)] + [vmem] * 14,
        out_specs=[vmem, vmem],
        scratch_shapes=[
            pltpu.VMEM((2, blocks, side + 8, LANES), jnp.float32),
            pltpu.VMEM((2, blocks, side, LANES), jnp.float32),
            pltpu.VMEM((KEPT, 2, 2, n, LANES), jnp.float32),
            pltpu.VMEM((3, positions, 8, LANES), jnp.float32),
        ] + slots,
        compiler_params=pltpu.CompilerParams(vmem_limit_bytes=40 * 1024 * 1024),
    )(offsets, *caps, *side_strips, *cap_sides, *quarters, probe, frames, forth, back)


def local(object_tiles, probe, frames, offsets):
    quarter = object_tiles[0]
    place = lax.axis_index("pos")
    turned = [quarter, round_ring(quarter, "pos", -1), round_ring(quarter, "pos", 2), round_ring(quarter, "pos", 1)]

    came = [
        up_and_down(quarter, 3, 0),
        up_and_down(turned[3], 0, 1),
        up_and_down(turned[1], 2, 3),
        up_and_down(turned[2], 1, 2),
    ]

    west = from_side(jnp.concatenate([piece[:, :, -MARGIN:] for piece in turned], axis=1), 1)
    east = from_side(jnp.concatenate([piece[:, :, :MARGIN] for piece in turned], axis=1), -1)

    def sides_of(pos):
        start = lax.rem(pos - place + 4, 4) * quarter.shape[1]
        both = [lax.dynamic_slice_in_dim(strip, start, MARGIN, axis=1) for strip in (west, east)]
        return jnp.concatenate(both, axis=2)

    cap_sides = (from_rows(sides_of(3), GC), from_rows(sides_of(0), -GC))

    def of_pos(order):
        return jnp.where(
            place < 2,
            jnp.where(place == 0, came[order[0]], came[order[1]]),
            jnp.where(place == 2, came[order[2]], came[order[3]]),
        )

    caps = (of_pos((1, 3, 2, 0)), of_pos((0, 1, 3, 2)))
    with_place = jnp.concatenate([offsets, jnp.full((1, offsets.shape[1]), place, jnp.int32)], axis=0)
    devices = lax.axis_size(TILE) * lax.axis_size("pos")
    positions = frames.shape[0]
    result, part = refine(with_place, caps, (west, east), cap_sides, turned, probe, frames, devices)
    parts = lax.all_to_all(part, TILE_POS, 0, 0, tiled=True)
    vmem = pl.BlockSpec(memory_space=pltpu.VMEM)
    shifts = pl.pallas_call(
        functools.partial(scale_kernel, count=positions * devices),
        out_shape=jax.ShapeDtypeStruct((2, positions), jnp.float32),
        in_specs=[vmem, vmem],
        out_specs=vmem,
    )(result, parts)
    return (shifts, result[2, :positions])


def solution(mesh):
    split = Mesh(
        mesh.devices.reshape(4, 4, 2, mesh.shape["pos"]), ("tile_0", "tile_1", "tile_2", "pos")
    )
    return jax.shard_map(
        local,
        mesh=split,
        in_specs=(P(TILE, None, "pos", None), P(), P(TILE_POS, None, None), P(None, TILE_POS)),
        out_specs=(P(None, TILE_POS), P(TILE_POS)),
        check_vma=False,
    )
```

```python
import functools
import math

import jax
import jax.numpy as jnp
import numpy as np
from jax import lax
from jax.experimental import pallas as pl
from jax.experimental.pallas import tpu as pltpu
from jax.sharding import Mesh
from jax.sharding import PartitionSpec as P

PROBE = 256
MARGIN = PROBE // 2
LANES = 128
CHUNK = 32
KEPT = 6
GC = 4
TILE = ("tile_0", "tile_1", "tile_2")
TILE_POS = ("tile_0", "tile_1", "tile_2", "pos")


def up_and_down(x, down, up):
    regions, across = lax.axis_size(TILE), lax.axis_size("pos")
    pairs = [(i * across + down, (i + GC) * across + down) for i in range(regions - GC)]
    pairs += [(i * across + up, (i - GC) * across + up) for i in range(GC, regions)]
    return lax.ppermute(x, TILE_POS, pairs)


def from_side(x, by):
    devices = lax.axis_size(TILE)
    pairs = [(i, i + by) for i in range(devices) if 0 <= i % GC + by < GC]
    return lax.ppermute(x, TILE, pairs)


def round_ring(x, axis, by):
    devices = lax.axis_size(axis)
    return lax.ppermute(x, axis, [(i, (i + by) % devices) for i in range(devices)])


def halved_tables(n):
    h = n // 2
    indices = np.arange(n, dtype=np.int32)
    angles = (indices[:, None] * indices[None, :] % n).astype(np.float32) * np.float32(2.0 * math.pi / n)
    factor = np.float32(1.0 / math.sqrt(n))
    cosine, sine = np.cos(angles) * factor, np.sin(angles) * factor
    forth = lambda c, s: np.block([[c, s], [-s, c]])
    back = lambda c, s: np.block([[c, -s], [s, c]])
    tables = []
    for kind, wide in ((forth, True), (back, False), (back, False), (forth, True)):
        for odd in range(2):
            c, s = (cosine[:h, odd::2], sine[:h, odd::2]) if wide else (cosine[odd::2, :h], sine[odd::2, :h])
            tables.append(kind(c, s))
    apart = np.zeros((n, n), np.float32)
    for odd in range(2):
        apart[2 * np.arange(h) + odd, odd * h + np.arange(h)] = 1.0
    return jnp.asarray(np.stack(tables + [apart]).astype(jnp.bfloat16))


def refine_kernel(place_ref, offsets_ref, north_ref, south_ref, side_west_ref, side_east_ref, caps_west_ref, caps_east_ref, *refs):
    quarter_refs = refs[:4]
    probe_ref, frames_ref, tables_ref, result_ref, part_ref, tile_ref, slant_ref, turned_ref, window_ref, sums_ref = refs[4:14]
    slots = refs[14:]
    n, h = PROBE, PROBE // 2
    groups = tile_ref.shape[2]
    side = groups * n
    pieces = len(quarter_refs) + 2
    positions = frames_ref.shape[0]
    exits, halves, fars, resids, inners, waves = (slots[2 * i:2 * i + 2] for i in range(6))

    def product(left, right):
        return jnp.dot(left, right, preferred_element_type=jnp.float32)

    def strip_of(piece, part, group):
        if piece in (0, pieces - 1):
            middle_ref = south_ref if piece else north_ref
            west_ref, east_ref, rows = caps_west_ref, caps_east_ref, pl.ds(LANES if piece else 0, LANES)
        else:
            middle_ref = quarter_refs[piece - 1]
            west_ref, east_ref, rows = side_west_ref, side_east_ref, pl.ds((piece - 1) * LANES, LANES)
        if group == 0:
            return jnp.concatenate([west_ref[part, rows, :], middle_ref[part, :, :LANES]], axis=1)
        if group == groups - 1:
            return jnp.concatenate([middle_ref[part, :, -LANES:], east_ref[part, rows, :]], axis=1)
        return middle_ref[part, :, pl.ds(group * n - LANES, n)]

    def rows_of(piece):
        if piece in (0, pieces - 1):
            return pl.ds(piece * LANES, LANES)
        turned = lax.rem(place_ref[0] + piece - 1, pieces - 2)
        return pl.ds(pl.multiple_of((turned + 1) * LANES, LANES), LANES)

    for part in range(2):
        for group in range(groups):
            for piece in range(0, pieces, 2):
                two = [strip_of(piece + i, part, group) for i in range(2)]
                apart = product(jnp.concatenate(two, axis=0), tables_ref[8])
                for i in range(2):
                    for odd in range(2):
                        tile_ref[part, odd, group, rows_of(piece + i), :] = apart[i * LANES:(i + 1) * LANES, odd * h:(odd + 1) * h]
    lane = lax.broadcasted_iota(jnp.int32, (LANES, LANES), 1)
    for part in range(2):
        for group in range(groups):
            for row in range(0, side, LANES):
                rows = pl.ds(row, LANES)
                even, odd = tile_ref[part, 0, group, rows, :], tile_ref[part, 1, group, rows, :]
                before = tile_ref[part, 1, max(group - 1, 0), rows, :]
                after = tile_ref[part, 0, min(group + 1, groups - 1), rows, :]
                slant_ref[part, 0, group, rows, :] = odd - pltpu.roll(jnp.where(lane == LANES - 1, before, odd), 1, 1)
                slant_ref[part, 1, group, rows, :] = pltpu.roll(jnp.where(lane == 0, after, even), LANES - 1, 1) - even

    def columns_of(position):
        start_col = offsets_ref[1, position]
        places = []
        for odd in range(2):
            first = (start_col - odd + 1) // 2
            group = first // LANES
            places.append((group, jnp.minimum(group + 1, groups - 1), first % LANES, lax.rem(start_col + odd, 2)))
        return places

    def cut(position, slot):
        start_row = offsets_ref[0, position]
        places = columns_of(position)
        held = lax.rem(position, KEPT)
        lane = lax.broadcasted_iota(jnp.int32, (2 * CHUNK, LANES), 1)

        def window(row, rows):
            for odd in range(2):
                group, following, rest, _ = places[odd]
                for part in range(2):
                    at = pl.ds(start_row - 1 + row, rows)
                    window_ref[held, part, odd, pl.ds(row, rows), :] = jnp.where(
                        lane[:rows] < rest, tile_ref[part, odd, following, at, :], tile_ref[part, odd, group, at, :]
                    )

        def piece(row_odd, row):
            rows = pl.ds(1 + row_odd + 2 * row, CHUNK, stride=2)
            for odd in range(2):
                _, _, rest, from_odd = places[odd]
                cols = pl.ds(odd * LANES, LANES)
                patch = [window_ref[held, part, odd, rows, :] for part in range(2)]
                probe = [
                    pltpu.roll(probe_ref[part, pl.ds(row_odd * h + row, CHUNK), pl.ds(pl.multiple_of(from_odd * h, h), h)], rest, 1) for part in range(2)
                ]
                for part in range(2):
                    turned_ref[held, part, row_odd, odd, pl.ds(row, CHUNK), :] = probe[part]
                exits[slot][row_odd, pl.ds(row, CHUNK), cols] = (probe[0] * patch[0] - probe[1] * patch[1]).astype(jnp.bfloat16)
                exits[slot][row_odd, pl.ds(h + row, CHUNK), cols] = (probe[0] * patch[1] + probe[1] * patch[0]).astype(jnp.bfloat16)

        pieces = [functools.partial(window, row, 2 * CHUNK) for row in range(0, n, 2 * CHUNK)]
        pieces.append(functools.partial(window, n, 8))
        for row in range(0, h, CHUNK):
            pieces += [functools.partial(piece, row_odd, row) for row_odd in range(2)]
        return pieces

    def forward(slot):
        def rows(i):
            even = product(tables_ref[0, pl.ds(i * h, h), :], exits[slot][0])
            odd = product(tables_ref[1, pl.ds(i * h, h), :], exits[slot][1])
            for first, both in ((0, even + odd), (h, even - odd)):
                for col_odd in range(2):
                    halves[slot][col_odd, first:first + h, i * h:(i + 1) * h] = both[:, col_odd * h:(col_odd + 1) * h].astype(jnp.bfloat16)

        def cols(i):
            fars[slot][i] = product(halves[slot][i], tables_ref[2 + i])

        return [functools.partial(f, i) for f in (rows, cols) for i in range(2)]

    def compare(position, slot):
        far_ref, resid_ref = fars[slot], resids[slot]
        total = [jnp.zeros((8, LANES), jnp.float32)]

        def piece(row):
            resid = []
            for lower in range(2):
                rows = pl.ds(lower * h + row, CHUNK)
                even = [far_ref[0, rows, pl.ds(part * h, h)] for part in range(2)]
                odd = [far_ref[1, rows, pl.ds(part * h, h)] for part in range(2)]
                for right in range(2):
                    far = [e - o if right else e + o for e, o in zip(even, odd)]
                    frame = frames_ref[position, rows, pl.ds(right * h, h)].astype(jnp.float32)
                    power = far[0] * far[0] + far[1] * far[1]
                    keep = 1.0 - frame * jnp.minimum(lax.rsqrt(power), 4.0)
                    total[0] += jnp.sum((power * (keep * keep)).reshape(CHUNK // 8, 8, LANES), axis=0)
                    resid.append([f * keep for f in far])
            for right in range(2):
                for part in range(2):
                    upper, lower = resid[right][part], resid[2 + right][part]
                    at = (pl.ds(part * h + row, CHUNK), pl.ds(right * h, h))
                    resid_ref[(0, *at)] = (upper + lower).astype(jnp.bfloat16)
                    resid_ref[(1, *at)] = (upper - lower).astype(jnp.bfloat16)
            if row + CHUNK == h:
                sums_ref[2, position] = total[0]

        return [functools.partial(piece, row) for row in range(0, h, CHUNK)]

    def backward(slot):
        def rows(i):
            inner = product(tables_ref[4 + i], resids[slot][i])
            left, right = inner[:, :h], inner[:, h:]
            for j, both in enumerate((left + right, left - right)):
                for part in range(2):
                    inners[slot][j, i * h:(i + 1) * h, part * h:(part + 1) * h] = both[part * h:(part + 1) * h].astype(jnp.bfloat16)

        def cols(i):
            waves[slot][i] = product(inners[slot][i], tables_ref[6 + i])

        return [functools.partial(f, i) for f in (rows, cols) for i in range(2)]

    def slopes(position, slot):
        start_row = offsets_ref[0, position]
        places = columns_of(position)
        held = lax.rem(position, KEPT)
        lane = lax.broadcasted_iota(jnp.int32, (CHUNK, LANES), 1)
        total = [jnp.zeros((8, LANES), jnp.float32)] * 2

        def piece(row_odd, row):
            first = start_row + row_odd + 2 * row
            for odd in range(2):
                group, following, rest, _ = places[odd]

                def cut_of(ref, part, start):
                    rows = pl.ds(start, CHUNK, stride=2)
                    return jnp.where(lane < rest, ref[part, odd, following, rows, :], ref[part, odd, group, rows, :])

                wave_re = waves[slot][odd, pl.ds(row_odd * h + row, CHUNK), pl.ds(0, h)]
                wave_im = waves[slot][odd, pl.ds(row_odd * h + row, CHUNK), pl.ds(h, h)]
                probe_re = turned_ref[held, 0, row_odd, odd, pl.ds(row, CHUNK), :]
                probe_im = turned_ref[held, 1, row_odd, odd, pl.ds(row, CHUNK), :]
                pull_re = wave_re * probe_re + wave_im * probe_im
                pull_im = wave_im * probe_re - wave_re * probe_im
                below = pl.ds(2 + row_odd + 2 * row, CHUNK, stride=2)
                above = pl.ds(row_odd + 2 * row, CHUNK, stride=2)
                down_re = window_ref[held, 0, odd, below, :] - window_ref[held, 0, odd, above, :]
                down_im = window_ref[held, 1, odd, below, :] - window_ref[held, 1, odd, above, :]
                total[0] += jnp.sum((pull_re * down_re + pull_im * down_im).reshape(CHUNK // 8, 8, LANES), axis=0)
                slant_re = cut_of(slant_ref, 0, first)
                slant_im = cut_of(slant_ref, 1, first)
                total[1] += jnp.sum((pull_re * slant_re + pull_im * slant_im).reshape(CHUNK // 8, 8, LANES), axis=0)
            if row_odd == 1 and row + CHUNK == h:
                sums_ref[0, position] = total[0]
                sums_ref[1, position] = total[1]

        return [functools.partial(piece, row_odd, row) for row_odd in range(2) for row in range(0, h, CHUNK)]

    def step(t, parity, stages):
        plain, matrix = [], []
        if 4 in stages: plain += slopes(t - 4, parity)
        if 2 in stages: plain += compare(t - 2, parity)
        if 0 in stages: plain += cut(t, parity)
        one = []
        if 1 in stages: one = forward(1 - parity)
        two = []
        if 3 in stages: two = backward(1 - parity)
        if one and two:
            matrix = [piece for both in zip(one, two) for piece in both]
        else:
            matrix = one + two
        done = 0
        for i, piece in enumerate(matrix):
            piece()
            upto = (i + 1) * len(plain) // len(matrix)
            for other in plain[done:upto]:
                other()
            done = upto
        for other in plain[done:]:
            other()

    for t in range(4):
        step(t, t % 2, range(t + 1))
    def pair(i, carry):
        t = 4 + 2 * i
        step(t, 0, range(5))
        step(t + 1, 1, range(5))
        return carry
    lax.fori_loop(0, (positions - 4) // 2, pair, 0)
    for t in range(positions, positions + 4):
        step(t, t % 2, range(t - positions + 1, 5))

    sums = jnp.sum(jnp.sum(sums_ref[...], axis=2), axis=2, keepdims=True)
    slope = 0.5 * sums[:2]
    part_ref[...] = jnp.full(part_ref.shape, jnp.sum(slope * slope))
    at = lax.broadcasted_iota(jnp.int32, (positions, LANES), 0) == lax.broadcasted_iota(jnp.int32, (positions, LANES), 1)
    for i, value in enumerate((slope[0], slope[1], sums[2] * (1.0 / (n * n)))):
        result_ref[i:i + 1, :] = jnp.sum(jnp.where(at, value, 0.0), axis=0, keepdims=True)


def scale_kernel(result_ref, parts_ref, shifts_ref, *, count):
    total = jnp.sum(jnp.sum(parts_ref[...], axis=0, keepdims=True)[:, :1])
    scale = 1.0 / jnp.sqrt(jnp.full((2, LANES), total * (1.0 / count) + 1e-06))
    shifts_ref[...] = (-result_ref[0:2, :] * scale)[:, :shifts_ref.shape[1]]


def refine(place, offsets, caps, side_strips, cap_strips, quarters, probe, frames, devices):
    n, h = PROBE, PROBE // 2
    positions = frames.shape[0]
    groups = (len(quarters) + 2) * LANES // n
    tables = halved_tables(n)
    apart = tables[8].astype(jnp.float32)
    probe = jnp.einsum("nr,pnm,mc->prc", apart, probe, apart, precision=lax.Precision.HIGHEST)
    vmem = pl.BlockSpec(memory_space=pltpu.VMEM)
    smem = pl.BlockSpec(memory_space=pltpu.SMEM)
    slots = []
    for dtype in (jnp.bfloat16, jnp.bfloat16, jnp.float32) * 2:
        slots += [pltpu.VMEM((2, n, n), dtype)] * 2
    return pl.pallas_call(
        refine_kernel,
        out_shape=[jax.ShapeDtypeStruct((8, LANES), jnp.float32), jax.ShapeDtypeStruct((devices, LANES), jnp.float32)],
        in_specs=[smem] * 2 + [vmem] * 13,
        out_specs=[vmem, vmem],
        scratch_shapes=[
            pltpu.VMEM((2, 2, groups, groups * n + 8, LANES), jnp.float32),
            pltpu.VMEM((2, 2, groups, groups * n, LANES), jnp.float32),
            pltpu.VMEM((KEPT, 2, 2, 2, h, LANES), jnp.float32),
            pltpu.VMEM((KEPT, 2, 2, n + 8, LANES), jnp.float32),
            pltpu.VMEM((3, positions, 8, LANES), jnp.float32),
        ] + slots,
        compiler_params=pltpu.CompilerParams(vmem_limit_bytes=40 * 1024 * 1024),
    )(place, offsets, *caps, *side_strips, *cap_strips, *quarters, probe, frames, tables)


def local(object_tiles, probe, frames, offsets):
    quarter = object_tiles[0]
    place = lax.axis_index("pos")
    turned = [quarter, round_ring(quarter, "pos", -1), round_ring(quarter, "pos", 2), round_ring(quarter, "pos", 1)]

    came = [
        up_and_down(quarter, 3, 0),
        up_and_down(turned[3], 0, 1),
        up_and_down(turned[1], 2, 3),
        up_and_down(turned[2], 1, 2),
    ]

    def strips(pieces):
        west = from_side(jnp.concatenate([piece[:, :, -MARGIN:] for piece in pieces], axis=1), 1)
        east = from_side(jnp.concatenate([piece[:, :, :MARGIN] for piece in pieces], axis=1), -1)
        return west, east

    def of_pos(order):
        return jnp.where(
            place < 2,
            jnp.where(place == 0, came[order[0]], came[order[1]]),
            jnp.where(place == 2, came[order[2]], came[order[3]]),
        )

    side_strips = strips(turned)
    caps = (of_pos((1, 3, 2, 0)), of_pos((0, 1, 3, 2)))
    cap_strips = strips(caps)
    devices = lax.axis_size(TILE) * lax.axis_size("pos")
    positions = frames.shape[0]
    result, part = refine(place.reshape(1), offsets, caps, side_strips, cap_strips, turned, probe, frames, devices)
    parts = lax.all_to_all(part, TILE_POS, 0, 0, tiled=True)
    vmem = pl.BlockSpec(memory_space=pltpu.VMEM)
    shifts = pl.pallas_call(
        functools.partial(scale_kernel, count=positions * devices),
        out_shape=jax.ShapeDtypeStruct((2, positions), jnp.float32),
        in_specs=[vmem, vmem],
        out_specs=vmem,
    )(result, parts)
    return (shifts, result[2, :positions])


def solution(mesh):
    split = Mesh(
        mesh.devices.reshape(4, 4, 2, mesh.shape["pos"]), ("tile_0", "tile_1", "tile_2", "pos")
    )
    return jax.shard_map(
        local,
        mesh=split,
        in_specs=(P(TILE, None, "pos", None), P(), P(TILE_POS, None, None), P(None, TILE_POS)),
        out_specs=(P(None, TILE_POS), P(TILE_POS)),
        check_vma=False,
    )
```

```python
import functools
import math

import jax
import jax.numpy as jnp
import numpy as np
from jax import lax
from jax.experimental import pallas as pl
from jax.experimental.pallas import tpu as pltpu
from jax.sharding import Mesh
from jax.sharding import PartitionSpec as P

PROBE = 256
MARGIN = PROBE // 2
LANES = 128
CHUNK = 32
KEPT = 6
GC = 4
TILE = ("tile_0", "tile_1", "tile_2")
TILE_POS = ("tile_0", "tile_1", "tile_2", "pos")


def up_and_down(x, down, up):
    regions, across = lax.axis_size(TILE), lax.axis_size("pos")
    pairs = [(i * across + down, (i + GC) * across + down) for i in range(regions - GC)]
    pairs += [(i * across + up, (i - GC) * across + up) for i in range(GC, regions)]
    return lax.ppermute(x, TILE_POS, pairs)


def from_side(x, by):
    devices = lax.axis_size(TILE)
    pairs = [(i, i + by) for i in range(devices) if 0 <= i % GC + by < GC]
    return lax.ppermute(x, TILE, pairs)


def round_ring(x, axis, by):
    devices = lax.axis_size(axis)
    return lax.ppermute(x, axis, [(i, (i + by) % devices) for i in range(devices)])


def halved_tables(n):
    h = n // 2
    indices = np.arange(n, dtype=np.int32)
    angles = (indices[:, None] * indices[None, :] % n).astype(np.float32) * np.float32(2.0 * math.pi / n)
    factor = np.float32(1.0 / math.sqrt(n))
    cosine, sine = np.cos(angles) * factor, np.sin(angles) * factor
    forth = lambda c, s: np.block([[c, s], [-s, c]])
    back = lambda c, s: np.block([[c, -s], [s, c]])
    tables = []
    for kind, wide in ((forth, True), (back, False), (back, False), (forth, True)):
        for odd in range(2):
            c, s = (cosine[:h, odd::2], sine[:h, odd::2]) if wide else (cosine[odd::2, :h], sine[odd::2, :h])
            tables.append(kind(c, s))
    apart = np.zeros((n, n), np.float32)
    for odd in range(2):
        apart[2 * np.arange(h) + odd, odd * h + np.arange(h)] = 1.0
    return jnp.asarray(np.stack(tables + [apart]).astype(jnp.bfloat16))


def refine_kernel(place_ref, offsets_ref, north_ref, south_ref, side_west_ref, side_east_ref, caps_west_ref, caps_east_ref, *refs):
    quarter_refs = refs[:4]
    probe_ref, frames_ref, tables_ref, result_ref, part_ref, tile_ref, slant_ref, turned_ref, window_ref, sums_ref, planes_ref = refs[4:15]
    slots = refs[15:]
    n, h = PROBE, PROBE // 2
    groups = tile_ref.shape[2]
    side = groups * n
    pieces = len(quarter_refs) + 2
    positions = frames_ref.shape[0]
    exits, halves, fars, resids, inners, waves = (slots[2 * i:2 * i + 2] for i in range(6))

    def product(left, right):
        return jnp.dot(left, right, preferred_element_type=jnp.float32)

    for part in range(2):
        apart = jnp.dot(
            probe_ref[part], tables_ref[8].astype(jnp.float32),
            precision=lax.Precision.HIGHEST, preferred_element_type=jnp.float32,
        )
        for odd in range(2):
            planes_ref[part, odd] = apart[:, odd * h:(odd + 1) * h]

    def strip_of(piece, part, group):
        if piece in (0, pieces - 1):
            middle_ref = south_ref if piece else north_ref
            west_ref, east_ref, rows = caps_west_ref, caps_east_ref, pl.ds(LANES if piece else 0, LANES)
        else:
            middle_ref = quarter_refs[piece - 1]
            west_ref, east_ref, rows = side_west_ref, side_east_ref, pl.ds((piece - 1) * LANES, LANES)
        if group == 0:
            return jnp.concatenate([west_ref[part, rows, :], middle_ref[part, :, :LANES]], axis=1)
        if group == groups - 1:
            return jnp.concatenate([middle_ref[part, :, -LANES:], east_ref[part, rows, :]], axis=1)
        return middle_ref[part, :, pl.ds(group * n - LANES, n)]

    def rows_of(piece):
        if piece in (0, pieces - 1):
            return pl.ds(piece * LANES, LANES)
        turned = lax.rem(place_ref[0] + piece - 1, pieces - 2)
        return pl.ds(pl.multiple_of((turned + 1) * LANES, LANES), LANES)

    for part in range(2):
        for group in range(groups):
            for piece in range(0, pieces, 2):
                two = [strip_of(piece + i, part, group) for i in range(2)]
                apart = product(jnp.concatenate(two, axis=0), tables_ref[8])
                for i in range(2):
                    for odd in range(2):
                        tile_ref[part, odd, group, rows_of(piece + i), :] = apart[i * LANES:(i + 1) * LANES, odd * h:(odd + 1) * h]
    lane = lax.broadcasted_iota(jnp.int32, (LANES, LANES), 1)
    for part in range(2):
        for group in range(groups):
            for row in range(0, side, LANES):
                rows = pl.ds(row, LANES)
                even, odd = tile_ref[part, 0, group, rows, :], tile_ref[part, 1, group, rows, :]
                before = tile_ref[part, 1, max(group - 1, 0), rows, :]
                after = tile_ref[part, 0, min(group + 1, groups - 1), rows, :]
                slant_ref[part, 0, group, rows, :] = odd - pltpu.roll(jnp.where(lane == LANES - 1, before, odd), 1, 1)
                slant_ref[part, 1, group, rows, :] = pltpu.roll(jnp.where(lane == 0, after, even), LANES - 1, 1) - even

    def columns_of(position):
        start_col = offsets_ref[1, position]
        places = []
        for odd in range(2):
            first = (start_col - odd + 1) // 2
            group = first // LANES
            places.append((group, jnp.minimum(group + 1, groups - 1), first % LANES, lax.rem(start_col + odd, 2)))
        return places

    def cut(position, slot):
        start_row = offsets_ref[0, position]
        places = columns_of(position)
        held = lax.rem(position, KEPT)
        lane = lax.broadcasted_iota(jnp.int32, (2 * CHUNK, LANES), 1)

        def window(row, rows):
            for odd in range(2):
                group, following, rest, _ = places[odd]
                for part in range(2):
                    at = pl.ds(start_row - 1 + row, rows)
                    window_ref[held, part, odd, pl.ds(row, rows), :] = jnp.where(
                        lane[:rows] < rest, tile_ref[part, odd, following, at, :], tile_ref[part, odd, group, at, :]
                    )

        def piece(row_odd, row):
            rows = pl.ds(1 + row_odd + 2 * row, CHUNK, stride=2)
            for odd in range(2):
                _, _, rest, from_odd = places[odd]
                cols = pl.ds(odd * LANES, LANES)
                patch = [window_ref[held, part, odd, rows, :] for part in range(2)]
                probe = [
                    pltpu.roll(planes_ref[part, from_odd, pl.ds(row_odd + 2 * row, CHUNK, stride=2), :], rest, 1) for part in range(2)
                ]
                for part in range(2):
                    turned_ref[held, part, row_odd, odd, pl.ds(row, CHUNK), :] = probe[part]
                exits[slot][row_odd, pl.ds(row, CHUNK), cols] = (probe[0] * patch[0] - probe[1] * patch[1]).astype(jnp.bfloat16)
                exits[slot][row_odd, pl.ds(h + row, CHUNK), cols] = (probe[0] * patch[1] + probe[1] * patch[0]).astype(jnp.bfloat16)

        pieces = [functools.partial(window, row, 2 * CHUNK) for row in range(0, n, 2 * CHUNK)]
        pieces.append(functools.partial(window, n, 8))
        for row in range(0, h, CHUNK):
            pieces += [functools.partial(piece, row_odd, row) for row_odd in range(2)]
        return pieces

    def forward(slot):
        def rows(i):
            even = product(tables_ref[0, pl.ds(i * h, h), :], exits[slot][0])
            odd = product(tables_ref[1, pl.ds(i * h, h), :], exits[slot][1])
            for first, both in ((0, even + odd), (h, even - odd)):
                for col_odd in range(2):
                    halves[slot][col_odd, first:first + h, i * h:(i + 1) * h] = both[:, col_odd * h:(col_odd + 1) * h].astype(jnp.bfloat16)

        def cols(i):
            fars[slot][i] = product(halves[slot][i], tables_ref[2 + i])

        return [functools.partial(f, i) for f in (rows, cols) for i in range(2)]

    def compare(position, slot):
        far_ref, resid_ref = fars[slot], resids[slot]
        total = [jnp.zeros((8, LANES), jnp.float32)]

        def piece(row):
            resid = []
            for lower in range(2):
                rows = pl.ds(lower * h + row, CHUNK)
                even = [far_ref[0, rows, pl.ds(part * h, h)] for part in range(2)]
                odd = [far_ref[1, rows, pl.ds(part * h, h)] for part in range(2)]
                for right in range(2):
                    far = [e - o if right else e + o for e, o in zip(even, odd)]
                    frame = frames_ref[position, rows, pl.ds(right * h, h)].astype(jnp.float32)
                    power = far[0] * far[0] + far[1] * far[1]
                    keep = 1.0 - frame * jnp.minimum(lax.rsqrt(power), 4.0)
                    total[0] += jnp.sum((power * (keep * keep)).reshape(CHUNK // 8, 8, LANES), axis=0)
                    resid.append([f * keep for f in far])
            for right in range(2):
                for part in range(2):
                    upper, lower = resid[right][part], resid[2 + right][part]
                    at = (pl.ds(part * h + row, CHUNK), pl.ds(right * h, h))
                    resid_ref[(0, *at)] = (upper + lower).astype(jnp.bfloat16)
                    resid_ref[(1, *at)] = (upper - lower).astype(jnp.bfloat16)
            if row + CHUNK == h:
                sums_ref[2, position] = total[0]

        return [functools.partial(piece, row) for row in range(0, h, CHUNK)]

    def backward(slot):
        def rows(i):
            inner = product(tables_ref[4 + i], resids[slot][i])
            left, right = inner[:, :h], inner[:, h:]
            for j, both in enumerate((left + right, left - right)):
                for part in range(2):
                    inners[slot][j, i * h:(i + 1) * h, part * h:(part + 1) * h] = both[part * h:(part + 1) * h].astype(jnp.bfloat16)

        def cols(i):
            waves[slot][i] = product(inners[slot][i], tables_ref[6 + i])

        return [functools.partial(f, i) for f in (rows, cols) for i in range(2)]

    def slopes(position, slot):
        start_row = offsets_ref[0, position]
        places = columns_of(position)
        held = lax.rem(position, KEPT)
        lane = lax.broadcasted_iota(jnp.int32, (CHUNK, LANES), 1)
        total = [jnp.zeros((8, LANES), jnp.float32)] * 2

        def piece(row_odd, row):
            first = start_row + row_odd + 2 * row
            for odd in range(2):
                group, following, rest, _ = places[odd]

                def cut_of(ref, part, start):
                    rows = pl.ds(start, CHUNK, stride=2)
                    return jnp.where(lane < rest, ref[part, odd, following, rows, :], ref[part, odd, group, rows, :])

                wave_re = waves[slot][odd, pl.ds(row_odd * h + row, CHUNK), pl.ds(0, h)]
                wave_im = waves[slot][odd, pl.ds(row_odd * h + row, CHUNK), pl.ds(h, h)]
                probe_re = turned_ref[held, 0, row_odd, odd, pl.ds(row, CHUNK), :]
                probe_im = turned_ref[held, 1, row_odd, odd, pl.ds(row, CHUNK), :]
                pull_re = wave_re * probe_re + wave_im * probe_im
                pull_im = wave_im * probe_re - wave_re * probe_im
                below = pl.ds(2 + row_odd + 2 * row, CHUNK, stride=2)
                above = pl.ds(row_odd + 2 * row, CHUNK, stride=2)
                down_re = window_ref[held, 0, odd, below, :] - window_ref[held, 0, odd, above, :]
                down_im = window_ref[held, 1, odd, below, :] - window_ref[held, 1, odd, above, :]
                total[0] += jnp.sum((pull_re * down_re + pull_im * down_im).reshape(CHUNK // 8, 8, LANES), axis=0)
                slant_re = cut_of(slant_ref, 0, first)
                slant_im = cut_of(slant_ref, 1, first)
                total[1] += jnp.sum((pull_re * slant_re + pull_im * slant_im).reshape(CHUNK // 8, 8, LANES), axis=0)
            if row_odd == 1 and row + CHUNK == h:
                sums_ref[0, position] = total[0]
                sums_ref[1, position] = total[1]

        return [functools.partial(piece, row_odd, row) for row_odd in range(2) for row in range(0, h, CHUNK)]

    def step(t, parity, stages):
        plain, matrix = [], []
        if 4 in stages: plain += slopes(t - 4, parity)
        if 2 in stages: plain += compare(t - 2, parity)
        if 0 in stages: plain += cut(t, parity)
        one = []
        if 1 in stages: one = forward(1 - parity)
        two = []
        if 3 in stages: two = backward(1 - parity)
        if one and two:
            matrix = [piece for both in zip(one, two) for piece in both]
        else:
            matrix = one + two
        done = 0
        for i, piece in enumerate(matrix):
            piece()
            upto = (i + 1) * len(plain) // len(matrix)
            for other in plain[done:upto]:
                other()
            done = upto
        for other in plain[done:]:
            other()

    for t in range(4):
        step(t, t % 2, range(t + 1))
    def pair(i, carry):
        t = 4 + 2 * i
        step(t, 0, range(5))
        step(t + 1, 1, range(5))
        return carry
    lax.fori_loop(0, (positions - 4) // 2, pair, 0)
    for t in range(positions, positions + 4):
        step(t, t % 2, range(t - positions + 1, 5))

    sums = jnp.sum(jnp.sum(sums_ref[...], axis=2), axis=2, keepdims=True)
    slope = 0.5 * sums[:2]
    part_ref[...] = jnp.full(part_ref.shape, jnp.sum(slope * slope))
    at = lax.broadcasted_iota(jnp.int32, (positions, LANES), 0) == lax.broadcasted_iota(jnp.int32, (positions, LANES), 1)
    for i, value in enumerate((slope[0], slope[1], sums[2] * (1.0 / (n * n)))):
        result_ref[i:i + 1, :] = jnp.sum(jnp.where(at, value, 0.0), axis=0, keepdims=True)


def scale_kernel(result_ref, parts_ref, shifts_ref, *, count):
    total = jnp.sum(jnp.sum(parts_ref[...], axis=0, keepdims=True)[:, :1])
    scale = 1.0 / jnp.sqrt(jnp.full((2, LANES), total * (1.0 / count) + 1e-06))
    shifts_ref[...] = (-result_ref[0:2, :] * scale)[:, :shifts_ref.shape[1]]


def refine(place, offsets, caps, side_strips, cap_strips, quarters, probe, frames, devices):
    n, h = PROBE, PROBE // 2
    positions = frames.shape[0]
    groups = (len(quarters) + 2) * LANES // n
    tables = halved_tables(n)
    vmem = pl.BlockSpec(memory_space=pltpu.VMEM)
    smem = pl.BlockSpec(memory_space=pltpu.SMEM)
    slots = []
    for dtype in (jnp.bfloat16, jnp.bfloat16, jnp.float32) * 2:
        slots += [pltpu.VMEM((2, n, n), dtype)] * 2
    return pl.pallas_call(
        refine_kernel,
        out_shape=[jax.ShapeDtypeStruct((8, LANES), jnp.float32), jax.ShapeDtypeStruct((devices, LANES), jnp.float32)],
        in_specs=[smem] * 2 + [vmem] * 13,
        out_specs=[vmem, vmem],
        scratch_shapes=[
            pltpu.VMEM((2, 2, groups, groups * n + 8, LANES), jnp.float32),
            pltpu.VMEM((2, 2, groups, groups * n, LANES), jnp.float32),
            pltpu.VMEM((KEPT, 2, 2, 2, h, LANES), jnp.float32),
            pltpu.VMEM((KEPT, 2, 2, n + 8, LANES), jnp.float32),
            pltpu.VMEM((3, positions, 8, LANES), jnp.float32),
            pltpu.VMEM((2, 2, n, h), jnp.float32),
        ] + slots,
        compiler_params=pltpu.CompilerParams(vmem_limit_bytes=40 * 1024 * 1024),
    )(place, offsets, *caps, *side_strips, *cap_strips, *quarters, probe, frames, tables)


def local(object_tiles, probe, frames, offsets):
    quarter = object_tiles[0]
    place = lax.axis_index("pos")
    turned = [quarter, round_ring(quarter, "pos", -1), round_ring(quarter, "pos", 2), round_ring(quarter, "pos", 1)]

    came = [
        up_and_down(quarter, 3, 0),
        up_and_down(turned[3], 0, 1),
        up_and_down(turned[1], 2, 3),
        up_and_down(turned[2], 1, 2),
    ]

    def strips(pieces):
        west = from_side(jnp.concatenate([piece[:, :, -MARGIN:] for piece in pieces], axis=1), 1)
        east = from_side(jnp.concatenate([piece[:, :, :MARGIN] for piece in pieces], axis=1), -1)
        return west, east

    def of_pos(order):
        return jnp.where(
            place < 2,
            jnp.where(place == 0, came[order[0]], came[order[1]]),
            jnp.where(place == 2, came[order[2]], came[order[3]]),
        )

    side_strips = strips(turned)
    caps = (of_pos((1, 3, 2, 0)), of_pos((0, 1, 3, 2)))
    cap_strips = strips(caps)
    devices = lax.axis_size(TILE) * lax.axis_size("pos")
    positions = frames.shape[0]
    result, part = refine(place.reshape(1), offsets, caps, side_strips, cap_strips, turned, probe, frames, devices)
    parts = lax.all_to_all(part, TILE_POS, 0, 0, tiled=True)
    vmem = pl.BlockSpec(memory_space=pltpu.VMEM)
    shifts = pl.pallas_call(
        functools.partial(scale_kernel, count=positions * devices),
        out_shape=jax.ShapeDtypeStruct((2, positions), jnp.float32),
        in_specs=[vmem, vmem],
        out_specs=vmem,
    )(result, parts)
    return (shifts, result[2, :positions])


def solution(mesh):
    split = Mesh(
        mesh.devices.reshape(4, 4, 2, mesh.shape["pos"]), ("tile_0", "tile_1", "tile_2", "pos")
    )
    return jax.shard_map(
        local,
        mesh=split,
        in_specs=(P(TILE, None, "pos", None), P(), P(TILE_POS, None, None), P(None, TILE_POS)),
        out_specs=(P(None, TILE_POS), P(TILE_POS)),
        check_vma=False,
    )
```

```python
import functools
import math

import jax
import jax.numpy as jnp
import numpy as np
from jax import lax
from jax.experimental import pallas as pl
from jax.experimental.pallas import tpu as pltpu
from jax.sharding import Mesh
from jax.sharding import PartitionSpec as P

PROBE = 256
MARGIN = PROBE // 2
LANES = 128
CHUNK = 32
KEPT = 6
GC = 4
TILE = ("tile_0", "tile_1", "tile_2")
TILE_POS = ("tile_0", "tile_1", "tile_2", "pos")


def up_and_down(x, down, up):
    regions, across = lax.axis_size(TILE), lax.axis_size("pos")
    pairs = [(i * across + down, (i + GC) * across + down) for i in range(regions - GC)]
    pairs += [(i * across + up, (i - GC) * across + up) for i in range(GC, regions)]
    return lax.ppermute(x, TILE_POS, pairs)


def from_side(x, by):
    devices = lax.axis_size(TILE)
    pairs = [(i, i + by) for i in range(devices) if 0 <= i % GC + by < GC]
    return lax.ppermute(x, TILE, pairs)


def round_ring(x, axis, by):
    devices = lax.axis_size(axis)
    return lax.ppermute(x, axis, [(i, (i + by) % devices) for i in range(devices)])


def halved_tables(n):
    h = n // 2
    indices = np.arange(n, dtype=np.int32)
    angles = (indices[:, None] * indices[None, :] % n).astype(np.float32) * np.float32(2.0 * math.pi / n)
    factor = np.float32(1.0 / math.sqrt(n))
    cosine, sine = np.cos(angles) * factor, np.sin(angles) * factor
    forth = lambda c, s: np.block([[c, s], [-s, c]])
    back = lambda c, s: np.block([[c, -s], [s, c]])
    tables = []
    for kind, wide in ((forth, True), (back, False), (back, False), (forth, True)):
        for odd in range(2):
            c, s = (cosine[:h, odd::2], sine[:h, odd::2]) if wide else (cosine[odd::2, :h], sine[odd::2, :h])
            tables.append(kind(c, s))
    apart = np.zeros((n, n), np.float32)
    for odd in range(2):
        apart[2 * np.arange(h) + odd, odd * h + np.arange(h)] = 1.0
    return jnp.asarray(np.stack(tables + [apart]).astype(jnp.bfloat16))


def refine_kernel(place_ref, offsets_ref, north_ref, south_ref, side_west_ref, side_east_ref, caps_west_ref, caps_east_ref, *refs):
    quarter_refs = refs[:4]
    probe_ref, frames_ref, tables_ref, result_ref, part_ref, tile_ref, slant_ref, turned_ref, window_ref, sums_ref, planes_ref = refs[4:15]
    slots = refs[15:]
    n, h = PROBE, PROBE // 2
    groups = tile_ref.shape[2]
    side = groups * n
    pieces = len(quarter_refs) + 2
    positions = frames_ref.shape[0]
    exits, halves, fars, resids, inners, waves = (slots[2 * i:2 * i + 2] for i in range(6))

    def product(left, right):
        return jnp.dot(left, right, preferred_element_type=jnp.float32)

    for part in range(2):
        rest, apart = probe_ref[part], None
        for _ in range(3):
            term = rest.astype(jnp.bfloat16)
            rest = rest - term.astype(jnp.float32)
            taken = product(term, tables_ref[8])
            apart = taken if apart is None else apart + taken
        for odd in range(2):
            planes_ref[part, odd, :n, :] = apart[:, odd * h:(odd + 1) * h]

    def strip_of(piece, part, group):
        if piece in (0, pieces - 1):
            middle_ref = south_ref if piece else north_ref
            west_ref, east_ref, rows = caps_west_ref, caps_east_ref, pl.ds(LANES if piece else 0, LANES)
        else:
            middle_ref = quarter_refs[piece - 1]
            west_ref, east_ref, rows = side_west_ref, side_east_ref, pl.ds((piece - 1) * LANES, LANES)
        if group == 0:
            return jnp.concatenate([west_ref[part, rows, :], middle_ref[part, :, :LANES]], axis=1)
        if group == groups - 1:
            return jnp.concatenate([middle_ref[part, :, -LANES:], east_ref[part, rows, :]], axis=1)
        return middle_ref[part, :, pl.ds(group * n - LANES, n)]

    def rows_of(piece):
        if piece in (0, pieces - 1):
            return pl.ds(piece * LANES, LANES)
        turned = lax.rem(place_ref[0] + piece - 1, pieces - 2)
        return pl.ds(pl.multiple_of((turned + 1) * LANES, LANES), LANES)

    for part in range(2):
        for group in range(groups):
            for piece in range(0, pieces, 6):
                two = [strip_of(piece + i, part, group) for i in range(6)]
                apart = product(jnp.concatenate(two, axis=0), tables_ref[8])
                for i in range(6):
                    for odd in range(2):
                        tile_ref[part, odd, group, rows_of(piece + i), :] = apart[i * LANES:(i + 1) * LANES, odd * h:(odd + 1) * h]
    lane = lax.broadcasted_iota(jnp.int32, (LANES, LANES), 1)
    for part in range(2):
        for group in range(groups):
            for row in range(0, side, LANES):
                rows = pl.ds(row, LANES)
                even, odd = tile_ref[part, 0, group, rows, :], tile_ref[part, 1, group, rows, :]
                before = tile_ref[part, 1, max(group - 1, 0), rows, :]
                after = tile_ref[part, 0, min(group + 1, groups - 1), rows, :]
                slant_ref[part, 0, group, rows, :] = odd - pltpu.roll(jnp.where(lane == LANES - 1, before, odd), 1, 1)
                slant_ref[part, 1, group, rows, :] = pltpu.roll(jnp.where(lane == 0, after, even), LANES - 1, 1) - even

    def columns_of(position):
        start_col = offsets_ref[1, position]
        places = []
        for odd in range(2):
            first = (start_col - odd + 1) // 2
            group = first // LANES
            places.append((group, jnp.minimum(group + 1, groups - 1), first % LANES, lax.rem(start_col + odd, 2)))
        return places

    def cut(position, slot):
        start_row = offsets_ref[0, position]
        places = columns_of(position)
        held = lax.rem(position, KEPT)
        lane = lax.broadcasted_iota(jnp.int32, (2 * CHUNK, LANES), 1)

        def window(row, rows):
            for odd in range(2):
                group, following, rest, _ = places[odd]
                for part in range(2):
                    at = pl.ds(start_row - 1 + row, rows)
                    window_ref[held, part, odd, pl.ds(row, rows), :] = jnp.where(
                        lane[:rows] < rest, tile_ref[part, odd, following, at, :], tile_ref[part, odd, group, at, :]
                    )

        def piece(row_odd, row):
            rows = pl.ds(1 + row_odd + 2 * row, CHUNK, stride=2)
            for odd in range(2):
                _, _, rest, from_odd = places[odd]
                cols = pl.ds(odd * LANES, LANES)
                patch = [window_ref[held, part, odd, rows, :] for part in range(2)]
                probe = [
                    pltpu.roll(planes_ref[part, from_odd, pl.ds(row_odd + 2 * row, CHUNK, stride=2), :], rest, 1) for part in range(2)
                ]
                for part in range(2):
                    turned_ref[held, part, row_odd, odd, pl.ds(row, CHUNK), :] = probe[part]
                exits[slot][row_odd, pl.ds(row, CHUNK), cols] = (probe[0] * patch[0] - probe[1] * patch[1]).astype(jnp.bfloat16)
                exits[slot][row_odd, pl.ds(h + row, CHUNK), cols] = (probe[0] * patch[1] + probe[1] * patch[0]).astype(jnp.bfloat16)

        pieces = [functools.partial(window, row, 2 * CHUNK) for row in range(0, n, 2 * CHUNK)]
        pieces.append(functools.partial(window, n, 8))
        for row in range(0, h, CHUNK):
            pieces += [functools.partial(piece, row_odd, row) for row_odd in range(2)]
        return pieces

    def forward(slot):
        def rows(i):
            even = product(tables_ref[0, pl.ds(i * h, h), :], exits[slot][0])
            odd = product(tables_ref[1, pl.ds(i * h, h), :], exits[slot][1])
            for first, both in ((0, even + odd), (h, even - odd)):
                for col_odd in range(2):
                    halves[slot][col_odd, first:first + h, i * h:(i + 1) * h] = both[:, col_odd * h:(col_odd + 1) * h].astype(jnp.bfloat16)

        def cols(i):
            fars[slot][i] = product(halves[slot][i], tables_ref[2 + i])

        return [functools.partial(f, i) for f in (rows, cols) for i in range(2)]

    def compare(position, slot):
        far_ref, resid_ref = fars[slot], resids[slot]
        total = [jnp.zeros((8, LANES), jnp.float32)]

        def piece(row):
            resid = []
            for lower in range(2):
                rows = pl.ds(lower * h + row, CHUNK)
                even = [far_ref[0, rows, pl.ds(part * h, h)] for part in range(2)]
                odd = [far_ref[1, rows, pl.ds(part * h, h)] for part in range(2)]
                for right in range(2):
                    far = [e - o if right else e + o for e, o in zip(even, odd)]
                    frame = frames_ref[position, rows, pl.ds(right * h, h)].astype(jnp.float32)
                    power = far[0] * far[0] + far[1] * far[1]
                    keep = 1.0 - frame * jnp.minimum(lax.rsqrt(power), 4.0)
                    total[0] += jnp.sum((power * (keep * keep)).reshape(CHUNK // 8, 8, LANES), axis=0)
                    resid.append([f * keep for f in far])
            for right in range(2):
                for part in range(2):
                    upper, lower = resid[right][part], resid[2 + right][part]
                    at = (pl.ds(part * h + row, CHUNK), pl.ds(right * h, h))
                    resid_ref[(0, *at)] = (upper + lower).astype(jnp.bfloat16)
                    resid_ref[(1, *at)] = (upper - lower).astype(jnp.bfloat16)
            if row + CHUNK == h:
                sums_ref[2, position] = total[0]

        return [functools.partial(piece, row) for row in range(0, h, CHUNK)]

    def backward(slot):
        def rows(i):
            inner = product(tables_ref[4 + i], resids[slot][i])
            left, right = inner[:, :h], inner[:, h:]
            for j, both in enumerate((left + right, left - right)):
                for part in range(2):
                    inners[slot][j, i * h:(i + 1) * h, part * h:(part + 1) * h] = both[part * h:(part + 1) * h].astype(jnp.bfloat16)

        def cols(i):
            waves[slot][i] = product(inners[slot][i], tables_ref[6 + i])

        return [functools.partial(f, i) for f in (rows, cols) for i in range(2)]

    def slopes(position, slot):
        start_row = offsets_ref[0, position]
        places = columns_of(position)
        held = lax.rem(position, KEPT)
        lane = lax.broadcasted_iota(jnp.int32, (CHUNK, LANES), 1)
        total = [jnp.zeros((8, LANES), jnp.float32)] * 2

        def piece(row_odd, row):
            first = start_row + row_odd + 2 * row
            for odd in range(2):
                group, following, rest, _ = places[odd]

                def cut_of(ref, part, start):
                    rows = pl.ds(start, CHUNK, stride=2)
                    return jnp.where(lane < rest, ref[part, odd, following, rows, :], ref[part, odd, group, rows, :])

                wave_re = waves[slot][odd, pl.ds(row_odd * h + row, CHUNK), pl.ds(0, h)]
                wave_im = waves[slot][odd, pl.ds(row_odd * h + row, CHUNK), pl.ds(h, h)]
                probe_re = turned_ref[held, 0, row_odd, odd, pl.ds(row, CHUNK), :]
                probe_im = turned_ref[held, 1, row_odd, odd, pl.ds(row, CHUNK), :]
                pull_re = wave_re * probe_re + wave_im * probe_im
                pull_im = wave_im * probe_re - wave_re * probe_im
                below = pl.ds(2 + row_odd + 2 * row, CHUNK, stride=2)
                above = pl.ds(row_odd + 2 * row, CHUNK, stride=2)
                down_re = window_ref[held, 0, odd, below, :] - window_ref[held, 0, odd, above, :]
                down_im = window_ref[held, 1, odd, below, :] - window_ref[held, 1, odd, above, :]
                total[0] += jnp.sum((pull_re * down_re + pull_im * down_im).reshape(CHUNK // 8, 8, LANES), axis=0)
                slant_re = cut_of(slant_ref, 0, first)
                slant_im = cut_of(slant_ref, 1, first)
                total[1] += jnp.sum((pull_re * slant_re + pull_im * slant_im).reshape(CHUNK // 8, 8, LANES), axis=0)
            if row_odd == 1 and row + CHUNK == h:
                sums_ref[0, position] = total[0]
                sums_ref[1, position] = total[1]

        return [functools.partial(piece, row_odd, row) for row_odd in range(2) for row in range(0, h, CHUNK)]

    def step(t, parity, stages):
        plain, matrix = [], []
        if 4 in stages: plain += slopes(t - 4, parity)
        if 2 in stages: plain += compare(t - 2, parity)
        if 0 in stages: plain += cut(t, parity)
        one = []
        if 1 in stages: one = forward(1 - parity)
        two = []
        if 3 in stages: two = backward(1 - parity)
        if one and two:
            matrix = [piece for both in zip(one, two) for piece in both]
        else:
            matrix = one + two
        done = 0
        for i, piece in enumerate(matrix):
            piece()
            upto = (i + 1) * len(plain) // len(matrix)
            for other in plain[done:upto]:
                other()
            done = upto
        for other in plain[done:]:
            other()

    for t in range(4):
        step(t, t % 2, range(t + 1))
    def pair(i, carry):
        t = 4 + 2 * i
        step(t, 0, range(5))
        step(t + 1, 1, range(5))
        return carry
    lax.fori_loop(0, (positions - 4) // 2, pair, 0)
    for t in range(positions, positions + 4):
        step(t, t % 2, range(t - positions + 1, 5))

    sums = jnp.sum(jnp.sum(sums_ref[...], axis=2), axis=2, keepdims=True)
    slope = 0.5 * sums[:2]
    part_ref[...] = jnp.full(part_ref.shape, jnp.sum(slope * slope))
    at = lax.broadcasted_iota(jnp.int32, (positions, LANES), 0) == lax.broadcasted_iota(jnp.int32, (positions, LANES), 1)
    for i, value in enumerate((slope[0], slope[1], sums[2] * (1.0 / (n * n)))):
        result_ref[i:i + 1, :] = jnp.sum(jnp.where(at, value, 0.0), axis=0, keepdims=True)


def scale_kernel(result_ref, parts_ref, shifts_ref, *, count):
    total = jnp.sum(jnp.sum(parts_ref[...], axis=0, keepdims=True)[:, :1])
    scale = 1.0 / jnp.sqrt(jnp.full((2, LANES), total * (1.0 / count) + 1e-06))
    shifts_ref[...] = (-result_ref[0:2, :] * scale)[:, :shifts_ref.shape[1]]


def refine(place, offsets, caps, side_strips, cap_strips, quarters, probe, frames, devices):
    n, h = PROBE, PROBE // 2
    positions = frames.shape[0]
    groups = (len(quarters) + 2) * LANES // n
    tables = halved_tables(n)
    vmem = pl.BlockSpec(memory_space=pltpu.VMEM)
    smem = pl.BlockSpec(memory_space=pltpu.SMEM)
    slots = []
    for dtype in (jnp.bfloat16, jnp.bfloat16, jnp.float32) * 2:
        slots += [pltpu.VMEM((2, n, n), dtype)] * 2
    return pl.pallas_call(
        refine_kernel,
        out_shape=[jax.ShapeDtypeStruct((8, LANES), jnp.float32), jax.ShapeDtypeStruct((devices, LANES), jnp.float32)],
        in_specs=[smem] * 2 + [vmem] * 13,
        out_specs=[vmem, vmem],
        scratch_shapes=[
            pltpu.VMEM((2, 2, groups, groups * n + 8, LANES), jnp.float32),
            pltpu.VMEM((2, 2, groups, groups * n, LANES), jnp.float32),
            pltpu.VMEM((KEPT, 2, 2, 2, h, LANES), jnp.float32),
            pltpu.VMEM((KEPT, 2, 2, n + 8, LANES), jnp.float32),
            pltpu.VMEM((3, positions, 8, LANES), jnp.float32),
            pltpu.VMEM((2, 2, n + 8, h), jnp.float32),
        ] + slots,
        compiler_params=pltpu.CompilerParams(vmem_limit_bytes=40 * 1024 * 1024),
    )(place, offsets, *caps, *side_strips, *cap_strips, *quarters, probe, frames, tables)


def local(object_tiles, probe, frames, offsets):
    quarter = object_tiles[0]
    place = lax.axis_index("pos")
    turned = [quarter, round_ring(quarter, "pos", -1), round_ring(quarter, "pos", 2), round_ring(quarter, "pos", 1)]

    came = [
        up_and_down(quarter, 3, 0),
        up_and_down(turned[3], 0, 1),
        up_and_down(turned[1], 2, 3),
        up_and_down(turned[2], 1, 2),
    ]

    def strips(pieces):
        west = from_side(jnp.concatenate([piece[:, :, -MARGIN:] for piece in pieces], axis=1), 1)
        east = from_side(jnp.concatenate([piece[:, :, :MARGIN] for piece in pieces], axis=1), -1)
        return west, east

    def of_pos(order):
        return jnp.where(
            place < 2,
            jnp.where(place == 0, came[order[0]], came[order[1]]),
            jnp.where(place == 2, came[order[2]], came[order[3]]),
        )

    side_strips = strips(turned)
    caps = (of_pos((1, 3, 2, 0)), of_pos((0, 1, 3, 2)))
    cap_strips = strips(caps)
    devices = lax.axis_size(TILE) * lax.axis_size("pos")
    positions = frames.shape[0]
    result, part = refine(place.reshape(1), offsets, caps, side_strips, cap_strips, turned, probe, frames, devices)
    parts = lax.all_to_all(part, TILE_POS, 0, 0, tiled=True)
    vmem = pl.BlockSpec(memory_space=pltpu.VMEM)
    shifts = pl.pallas_call(
        functools.partial(scale_kernel, count=positions * devices),
        out_shape=jax.ShapeDtypeStruct((2, positions), jnp.float32),
        in_specs=[vmem, vmem],
        out_specs=vmem,
    )(result, parts)
    return (shifts, result[2, :positions])


def solution(mesh):
    split = Mesh(
        mesh.devices.reshape(4, 4, 2, mesh.shape["pos"]), ("tile_0", "tile_1", "tile_2", "pos")
    )
    return jax.shard_map(
        local,
        mesh=split,
        in_specs=(P(TILE, None, "pos", None), P(), P(TILE_POS, None, None), P(None, TILE_POS)),
        out_specs=(P(None, TILE_POS), P(TILE_POS)),
        check_vma=False,
    )
```
